32 devices in a mesh: ga: 4 (over y, x), ty: 2 (over core), tx: 4 (over z).
Axes of the slice: x: 2, y: 2, z: 4, core: 2. Of those that a mesh axis runs over, the one named last changes fastest.
Arguments:
- snapshots: bfloat16 [1536, 32, 4096], P(('ga', 'ty', 'tx')), may hold values from -6 to 6
- counts: int32 [1536], P('ga'), may hold values from 1 to 4, as said below
- enc_weight: bfloat16 [64, 32, 5, 5], replicated, may hold values from -0.21875 to 0.21875
- enc_bias: bfloat16 [64], replicated, may hold values from -3 to 3
- dec_weight: bfloat16 [32, 64, 5, 5], replicated, may hold values from -0.3125 to 0.3125
- dec_bias: bfloat16 [32], replicated, may hold values from -3 to 3
- cotangent: bfloat16 [1536, 32, 2, 4, 512], P('ga', None, 'ty', 'tx'), may hold values from -6 to 6
Outputs:
- decoded: bfloat16 [1536, 32, 2, 4, 512], P('ga', None, 'ty', 'tx')
- input_grad: bfloat16 [1536, 32, 4096], P(('ga', 'ty', 'tx'))
- enc_weight_grad: float32 [25, 2048], replicated
- enc_bias_grad: float32 [64], replicated
- dec_weight_grad: float32 [25, 2048], replicated
- dec_bias_grad: float32 [32], replicated
The draws below stay inside these ranges and needn't reach their ends.
Inputs may be any that keep to these rules, and one draw needn't show every extreme that they name: `counts`: each entry is 1, 2 or 4.
All inputs are finite; a program needn't handle non-finite values.
Results may differ from the reference program's by a relative error of at most 0.0056.
Values may be sent and summed in bfloat16 or wider, within the bound.
A program may use at most 320 MiB of HBM per device.

```python
import jax
import jax.numpy as jnp
from jax import lax

C_IN = 32
C_MID = 64
GRID = 64
SNAP_DEV = 48
SNAPS = 1536
TILE_ROWS = 32
TILE_COLS = 16
N_TY = 2
N_TX = 4


def draw_counts(key, part):
    key = jax.random.fold_in(key, 7)
    powers = jax.random.randint(key, (SNAPS,), 0, 3).astype(jnp.int32)
    values = jnp.left_shift(jnp.ones_like(powers), powers)
    values = values.at[0].set(4).at[SNAPS - 1].set(1)
    return values.astype(jnp.int32)


def block_levels(rng, extent, cuts, smallest, largest):
    gain, own = 1.0, jax.random.fold_in(rng, 6)
    for position, blocks in cuts:
        draws = jnp.exp(jax.random.uniform(jax.random.fold_in(own, position), (blocks,), jnp.float32, smallest / len(cuts), largest / len(cuts)))
        gain = gain * jnp.repeat(draws, extent[position] // blocks).reshape([-1 if axis == position else 1 for axis in range(len(extent))])
    return gain


def bell_draw(stream_key, dims, spread, reach, cuts=(), kind=jnp.bfloat16):
    level = block_levels(stream_key, dims, cuts, -0.22, 0.18) if cuts else 1.0
    result = jax.random.normal(stream_key, dims, jnp.float32) * spread * level
    return jnp.minimum(jnp.maximum(result, -reach), reach).astype(kind)


def setup_inputs(seed: int = 0) -> dict:
    keys = jax.random.split(jax.random.key(seed), 8)
    snapshots = bell_draw(keys[0], (SNAPS, C_IN, GRID * GRID), 1.0, 6.0, ((0, 32),))
    counts = draw_counts(jax.random.fold_in(keys[7], 71), 0)
    enc_weight = bell_draw(keys[2], (C_MID, C_IN, 5, 5), (C_IN * 25) ** -0.5, 0.21875)
    enc_bias = bell_draw(keys[3], (C_MID,), 0.5, 3.0)
    dec_weight = bell_draw(keys[4], (C_IN, C_MID, 5, 5), (C_MID * 25 // 4) ** -0.5, 0.3125)
    dec_bias = bell_draw(keys[5], (C_IN,), 0.5, 3.0)
    cotangent = bell_draw(keys[6], (SNAPS, C_IN, N_TY, N_TX, TILE_ROWS * TILE_COLS), 1.0, 6.0, ((0, 4), (2, 2), (3, 4)))
    return {"snapshots": snapshots, "counts": counts, "enc_weight": enc_weight, "enc_bias": enc_bias, "dec_weight": dec_weight, "dec_bias": dec_bias, "cotangent": cotangent}


@jax.custom_vjp
def low(v):
    return lax.optimization_barrier(v.astype(jnp.bfloat16)).astype(jnp.float32)

@jax.custom_vjp
def low_back(v):
    return v

def low_keep(v):
    return (low(v), None)

def low_pass(kept, grad):
    return (grad,)

def back_keep(v):
    return (v, None)

def back_low(kept, grad):
    return (low(grad),)
low.defvjp(low_keep, low_pass)
low_back.defvjp(back_keep, back_low)
FORWARD_DIMS = ('NCHW', 'OIHW', 'NCHW')

def autoencode(images, keep_mask, enc_weight, enc_bias, dec_weight, dec_bias):
    masked = images * keep_mask
    pre_enc = lax.conv_general_dilated(masked, enc_weight, (2, 2), ((2, 2), (2, 2)), dimension_numbers=FORWARD_DIMS, precision=lax.Precision.HIGHEST)
    pre_enc = low_back(pre_enc + enc_bias[None, :, None, None])
    hidden = low_back(low(jax.nn.elu(pre_enc)))
    pre_dec = lax.conv_general_dilated(hidden, dec_weight, (1, 1), ((2, 3), (2, 3)), lhs_dilation=(2, 2), dimension_numbers=FORWARD_DIMS, precision=lax.Precision.HIGHEST)
    pre_dec = low_back(pre_dec + dec_bias[None, :, None, None])
    return jax.nn.elu(pre_dec) * keep_mask

def reference(snapshots, counts, enc_weight, enc_bias, dec_weight, dec_bias, cotangent):
    blocks = SNAPS // SNAP_DEV
    images = snapshots.reshape(blocks, SNAP_DEV, C_IN, GRID, GRID)
    whole_tangent = cotangent.reshape(SNAPS, C_IN, N_TY, N_TX, TILE_ROWS, TILE_COLS)
    whole_tangent = whole_tangent.transpose(0, 1, 2, 4, 3, 5).reshape(SNAPS, C_IN, GRID, GRID)
    tangents = whole_tangent.reshape(blocks, SNAP_DEV, C_IN, GRID, GRID)
    block_counts = counts.reshape(blocks, SNAP_DEV)
    weights = (enc_weight.astype(jnp.float32), enc_bias.astype(jnp.float32), dec_weight.astype(jnp.float32), dec_bias.astype(jnp.float32))
    field_index = jnp.arange(C_IN, dtype=jnp.int32) // (C_IN // 4)

    def block_step(totals, item):
        block_images, block_count, block_tangent = item
        keep_mask = (field_index[None, :] < block_count[:, None]).astype(jnp.float32)[:, :, None, None]

        def forward(images_f, enc_w, enc_b, dec_w, dec_b):
            return autoencode(images_f, keep_mask, enc_w, enc_b, dec_w, dec_b)
        decoded, pullback = jax.vjp(forward, block_images.astype(jnp.float32), *weights)
        grads = pullback(block_tangent.astype(jnp.float32))
        totals = tuple((total + grad for total, grad in zip(totals, grads[1:])))
        return (totals, (decoded.astype(jnp.bfloat16), grads[0].astype(jnp.bfloat16)))
    start = tuple((jnp.zeros_like(weight) for weight in weights))
    sums, (decoded, input_grad) = lax.scan(block_step, start, (images, block_counts, tangents))
    decoded = decoded.reshape(SNAPS, C_IN, N_TY, TILE_ROWS, N_TX, TILE_COLS)
    decoded = decoded.transpose(0, 1, 2, 4, 3, 5).reshape(SNAPS, C_IN, N_TY, N_TX, TILE_ROWS * TILE_COLS)
    input_grad = input_grad.reshape(SNAPS, C_IN, GRID * GRID)
    enc_weight_grad = sums[0].transpose(2, 3, 0, 1).reshape(25, C_MID * C_IN)
    dec_weight_grad = sums[2].transpose(2, 3, 0, 1).reshape(25, C_IN * C_MID)
    return (decoded, input_grad, enc_weight_grad, sums[1], dec_weight_grad, sums[3])
```

```python
import functools

import jax
import jax.numpy as jnp
import ml_dtypes
import numpy as np
from jax import lax
from jax.experimental import pallas as pl
from jax.experimental.pallas import tpu as pltpu
from jax.sharding import PartitionSpec as P


FINE = 32
MID = 64
GRID = 64
COARSE = 32
LANES = 128
TAPS = 5
ROWS = TAPS * 2 * FINE
COLS = 3 * MID
ONES = 16
UNIT = 4
BF = jnp.bfloat16
F32 = jnp.float32
VMEM_BYTES = 56 * 1024 * 1024


class Plan:
    def __init__(self, tiles):
        self.tiles = tiles
        self.width = COARSE // tiles
        self.vregs = COARSE * self.width // LANES
        self.rows = LANES // self.width
        self.packet = 2 * self.vregs * LANES + LANES


def one(matrix):
    return matrix.astype(ml_dtypes.bfloat16)


def image_split():
    out = np.zeros((4, 2, 32, 2, 2, 2, 4, 32), np.float32)
    for m in range(4):
        for pr in range(2):
            for j in range(32):
                for pc in range(2):
                    out[m, pr, j, pc, pr, pc, m, j] = 1
    return one(out.reshape(512, 512))


def tile_split(plan):
    n, w = plan.rows, plan.width
    out = np.zeros((n, 2, w, 2, 2, 2, n, w), np.float32)
    for i in range(n):
        for pr in range(2):
            for j in range(w):
                for pc in range(2):
                    out[i, pr, j, pc, pr, pc, i, j] = 1
    return one(out.reshape(512, 512))


def to_tiles(plan):
    halves = 2 // plan.vregs
    out = np.zeros((halves, 4, 4, plan.tiles, plan.width, plan.tiles, halves, 4, 4, plan.width), np.float32)
    for r in range(halves):
        for u in range(4):
            for m in range(4):
                for t in range(plan.tiles):
                    for j in range(plan.width):
                        out[r, u, m, t, j, t, r, m, u, j] = 1
    size = halves * 4 * LANES
    return one(out.reshape(size, size))


def edge_pick(plan, swap):
    v, n, w = plan.vregs, plan.rows, plan.width
    out = np.zeros((2, v, n, w, 2, v, 2, n), np.float32)
    for p in range(2):
        for q in range(v):
            for i in range(n):
                for edge in range(2):
                    out[p, q, i, (w - 1) * (edge ^ swap), p, q, edge, i] = 1
    return one(out.reshape(2 * v * LANES, LANES))


def column_shifts(plan):
    v, n, w = plan.vregs, plan.rows, plan.width
    out = np.zeros((2, v, 2, LANES, 2, n, w), np.float32)
    for p in range(2):
        for q in range(v):
            for i in range(n):
                for j in range(w):
                    if j < w - 1:
                        out[p, q, 0, i * w + j + 1, 0, i, j] = 1
                    else:
                        out[p, q, 1, ((p * v + q) * 2 + 0) * n + i, 0, i, j] = 1
                    if j > 0:
                        out[p, q, 0, i * w + j - 1, 1, i, j] = 1
                    else:
                        out[p, q, 1, ((p * v + q) * 2 + 1) * n + i, 1, i, j] = 1
    return one(out.reshape(2 * v, 2 * LANES, 2 * LANES))


def dot(a, b):
    return jnp.dot(a, b, preferred_element_type=F32)


def dot_nt(a, b):
    return lax.dot_general(a, b, (((1,), (1,)), ((), ())), preferred_element_type=F32)


def lane_of(rows):
    return lax.broadcasted_iota(jnp.int32, (rows, LANES), 1)


def turn(x, by):
    return pltpu.roll(x, (-by) % LANES, 1)


def shift_rows(pieces, d, halves, inner, step):
    lane = lane_of(pieces[0].shape[0])
    out = []
    for r in range(halves):
        for u in range(inner):
            if 0 <= u + d < inner:
                out.append(pieces[r * inner + u + d])
            elif d > 0:
                here = turn(pieces[r * inner], step)
                after = turn(pieces[(r + 1) * inner], step) if r + 1 < halves else 0.0
                out.append(jnp.where(lane < LANES - step, here, after))
            else:
                here = turn(pieces[r * inner + inner - 1], -step)
                before = turn(pieces[r * inner - 1], -step) if r else 0.0
                out.append(jnp.where(lane >= step, here, before))
    return out


def shift_cols(x, d, width):
    j = lane_of(x.shape[0]) & (width - 1)
    return jnp.where(j < width - 1 if d > 0 else j >= 1, turn(x, d), 0.0)


def tap_of(t):
    return t % 2, t // 2 - 1


def up_rows(q, parity, halves, inner, step):
    total = None
    for t in range(parity, TAPS, 2):
        d = -tap_of(t)[1]
        part = q[t] if d == 0 else shift_rows(q[t], d, halves, inner, step)
        total = part if total is None else [a + b for a, b in zip(total, part)]
    return total


def kept(count):
    return lax.broadcasted_iota(jnp.int32, (FINE, LANES), 0) // (FINE // 4) < count


def encode_kernel(plan, ns, chunk, nb, carried, place, counts, x, split, tiles, edges, weights_t, bias, *rest):
    refs, rest = rest[:carried], rest[carried:]
    send, (slope, phases, there, *rest) = rest[: plan.tiles], rest[plan.tiles :]
    refs, (lx, rows, lt, lc, stage) = (*refs, *rest[:carried]), rest[carried:]
    there[0], there[1] = place[0], place[1]
    first = (place[0] * plan.tiles + place[1]) * ns + chunk + pl.program_id(0) * nb
    tx = place[1]
    width, vregs, per = plan.width, plan.vregs, 8 // plan.vregs
    if carried:
        refs[-1][...] = refs[-2][...]
    for n in range(nb):
        keep = kept(counts[first + n]).astype(BF)
        for i in range(COARSE):
            r, m, u = i // 16, i % 16 // 4, i % 4
            lx[r * 4 + u, n, :, m * LANES : (m + 1) * LANES] = x[n, :, i * LANES : (i + 1) * LANES] * keep
    y = dot(lx[...].reshape(8 * nb * FINE, 512), split[...])
    for n in range(nb):
        for ph in range(4):
            pr, pc = ph // 2, ph % 2
            pieces = [
                y[(v * nb + n) * FINE : (v * nb + n + 1) * FINE, ph * LANES : (ph + 1) * LANES] for v in range(8)
            ]
            for v in range(8):
                phases[n, ph * FINE : (ph + 1) * FINE, v * LANES : (v + 1) * LANES] = pieces[v].astype(BF)
            for t in range(pr, TAPS, 2):
                d = tap_of(t)[1]
                moved = shift_rows(pieces, d, 2, 4, COARSE)
                at = (t * 2 + pc) * FINE
                for v in range(8):
                    rows[at : at + FINE, v * LANES : (v + 1) * LANES] = moved[v].astype(BF)
        s = dot(weights_t[...], rows[...])
        for v in range(8):
            cut = slice(v * LANES, (v + 1) * LANES)
            pre = s[MID : 2 * MID, cut] + bias[...]
            pre += shift_cols(s[:MID, cut], -1, COARSE) + shift_cols(s[2 * MID :, cut], 1, COARSE)
            e = jnp.exp(jnp.minimum(pre, 0.0))
            slope[n, :, cut] = e.astype(BF)
            hidden = jnp.where(pre > 0, pre, e - 1.0).astype(BF)
            w, at = v // per, v % per
            lt[w, n, :, at * LANES : (at + 1) * LANES] = hidden
    z = dot(lt[...].reshape(vregs * nb * MID, per * LANES), tiles[...])
    j = lane_of(MID) & (width - 1)
    for n in range(nb):
        for w in range(vregs):
            at = (w * nb + n) * MID
            main = [z[at : at + MID, t * LANES : (t + 1) * LANES] for t in range(plan.tiles)]
            cut = slice((n % 2 * vregs + w) * LANES, (n % 2 * vregs + w + 1) * LANES)
            for t in range(plan.tiles):
                stage[t, n // 2, :, cut] = main[t].astype(BF)
                left = main[t - 1] if t else 0.0
                right = main[t + 1] if t + 1 < plan.tiles else 0.0
                rim = jnp.where(j == 0, right, jnp.where(j == width - 1, left, 0.0))
                lc[t, n // 2, :, cut] = rim.astype(BF)
    rims = dot(lc[...].reshape(plan.tiles * nb // 2 * MID, 2 * vregs * LANES), edges[...])
    for t in range(plan.tiles):
        for pair in range(nb // 2):
            at = (t * nb // 2 + pair) * MID
            stage[t, pair, :, 2 * vregs * LANES :] = rims[at : at + MID].astype(BF)
    for k in range(plan.tiles):
        send[k][...] = stage[tx ^ k]


def decode_kernel(plan, ns, chunk, nb, chained, place, *refs):
    parts, refs = refs[: plan.tiles], refs[plan.tiles :]
    counts, own, other, before, split, join, shifts, edges, weights, weights_t, bias = refs[:11]
    home, away, total, *refs = refs[11 + chained :]
    sends, (lcot, cols, rows, ldec, lc, got, send) = refs[: plan.tiles], refs[plan.tiles :]
    ty, part, step = place[0], pl.program_id(0), pl.program_id(1)
    upper = ty == 0
    first = (place[1] ^ part) * ns + chunk + step * nb
    width, vregs = plan.width, plan.vregs
    edge_at = 2 * vregs * LANES
    masks = [kept(counts[first + n]) for n in range(nb)]

    @pl.when((part == 0) & (step == 0))
    def _():
        total[...] = before[...]

    for k in range(plan.tiles):

        @pl.when(part == k)
        def _():
            got[...] = parts[k][...]

    half = 2 // vregs
    span = 4 // half
    for n in range(nb):
        keep = masks[n].astype(BF)
        for k in range(span):
            cut = slice(k * LANES, (k + 1) * LANES)
            mine, theirs = own[0, 0, n, :, cut] * keep, other[0, n, :, cut] * keep
            for side in range(2):
                k_to = k + side % half * span
                lcot[side // half, n, :, k_to * LANES : (k_to + 1) * LANES] = (
                    jnp.where(upper, mine, theirs) if side == 0 else jnp.where(upper, theirs, mine)
                )
    c = dot(lcot[...].reshape(vregs * nb * FINE, 512), split[...])
    for p in range(2):
        for w in range(vregs):
            slot = p * vregs + w
            at = slice(slot * LANES, (slot + 1) * LANES)
            both = jnp.concatenate([got[:, :, at], got[:, :, edge_at:]], axis=2)
            moved = dot(both.reshape(nb // 2 * MID, 2 * LANES), shifts[slot]).astype(BF)
            for pair in range(nb // 2):
                lanes = slice(((2 * pair + p) * vregs + w) * LANES, ((2 * pair + p) * vregs + w + 1) * LANES)
                sub = slice(pair * MID, (pair + 1) * MID)
                cols[:MID, lanes] = moved[sub, :LANES]
                cols[MID : 2 * MID, lanes] = got[pair, :, at]
                cols[2 * MID : COLS, lanes] = moved[sub, LANES:]
    cols[COLS:, :] = jnp.ones((ONES, nb * vregs * LANES), BF)
    q = dot(weights[...], cols[:COLS, :])
    for n in range(nb):
        for pr in range(2):
            reg = {
                t: [
                    q[t * MID : (t + 1) * MID, (n * vregs + w) * LANES : (n * vregs + w + 1) * LANES]
                    for w in range(vregs)
                ]
                for t in range(pr, TAPS, 2)
            }
            pre = [x + bias[...] for x in up_rows(reg, pr, vregs, 1, width)]
            grads = []
            for w in range(vregs):
                e = jnp.exp(jnp.minimum(pre[w], 0.0))
                at = (w * nb + n) * FINE
                tangent = jnp.concatenate(
                    [
                        c[at : at + FINE, (2 * pr + pc) * LANES : (2 * pr + pc + 1) * LANES]
                        for pc in range(2)
                    ],
                    axis=0,
                )
                grads.append(tangent * e)
                out = jnp.where(pre[w] > 0, pre[w], e - 1.0).astype(BF)
                for pc in range(2):
                    cut = slice((2 * pr + pc) * LANES, (2 * pr + pc + 1) * LANES)
                    ldec[w, n, :, cut] = out[pc * FINE : (pc + 1) * FINE]
            for t in range(pr, TAPS, 2):
                moved = grads if t // 2 == 1 else shift_rows(grads, tap_of(t)[1], vregs, 1, width)
                for w in range(vregs):
                    lanes = slice((n * vregs + w) * LANES, (n * vregs + w + 1) * LANES)
                    rows[t * MID : (t + 1) * MID, lanes] = moved[w].astype(BF)
    nat = dot(ldec[...].reshape(vregs * nb * FINE, 512), join[...])
    for n in range(nb):
        for k in range(span):
            sides = []
            for side in range(2):
                at = (side // half * nb + n) * FINE
                k_from = k + side % half * span
                sides.append(jnp.where(masks[n], nat[at : at + FINE, k_from * LANES : (k_from + 1) * LANES], 0.0))
            cut = slice(k * LANES, (k + 1) * LANES)
            home[0, 0, n, :, cut] = jnp.where(upper, sides[0], sides[1]).astype(BF)
            away[0, n, :, cut] = jnp.where(upper, sides[1], sides[0]).astype(BF)
    s = dot(weights_t[...], rows[...])
    j = lane_of(MID) & (width - 1)
    for n in range(nb):
        for w in range(vregs):
            lanes = slice((n * vregs + w) * LANES, (n * vregs + w + 1) * LANES)
            behind, here, ahead = s[:MID, lanes], s[MID : 2 * MID, lanes], s[2 * MID :, lanes]
            grad = here + shift_cols(behind, -1, width) + shift_cols(ahead, 1, width)
            slot = n % 2 * vregs + w
            cut = slice(slot * LANES, (slot + 1) * LANES)
            send[n // 2, :, cut] = grad.astype(BF)
            lc[n // 2, :, cut] = jnp.where(j == 0, ahead, behind).astype(BF)
    rims = dot(lc[...].reshape(nb // 2 * MID, edge_at), edges[...])
    for pair in range(nb // 2):
        send[pair, :, edge_at:] = rims[pair * MID : (pair + 1) * MID].astype(BF)
    total[:, : COLS + ONES] += dot_nt(rows[...], cols[...])
    for k in range(plan.tiles):

        @pl.when(part == k)
        def _():
            sends[k][...] = send[...]


def back_kernel(plan, ns, chunk, nb, chained, place, counts, *refs):
    parts, refs = refs[: plan.tiles], refs[plan.tiles :]
    slope, phases, before, spread, untile, join, weights = refs[:7]
    grad, total, taps, got, lu, cols, rows, lo = refs[7 + chained :]
    step = pl.program_id(0)
    first = (place[0] * plan.tiles + place[1]) * ns + chunk + step * nb
    tx = place[1]
    width, vregs, per = plan.width, plan.vregs, 8 // plan.vregs
    edge_at = 2 * vregs * LANES

    @pl.when(step == 0)
    def _():
        total[...] = before[...]

    for k in range(plan.tiles):
        got[tx ^ k] = parts[k][...]
    rims = dot(got[:, :, :, edge_at:].reshape(plan.tiles * nb // 2 * MID, LANES), spread[...])
    j = lane_of(MID) & (width - 1)
    for n in range(nb):
        for w in range(vregs):
            slot = n % 2 * vregs + w
            cut = slice(slot * LANES, (slot + 1) * LANES)
            rim = [
                rims[(t * nb // 2 + n // 2) * MID : (t * nb // 2 + n // 2 + 1) * MID, cut] for t in range(plan.tiles)
            ]
            for t in range(plan.tiles):
                main = got[t, n // 2, :, cut].astype(F32)
                if t + 1 < plan.tiles:
                    main += jnp.where(j == width - 1, rim[t + 1], 0.0)
                if t:
                    main += jnp.where(j == 0, rim[t - 1], 0.0)
                lu[w, n, :, t * LANES : (t + 1) * LANES] = main.astype(BF)
    g = dot(lu[...].reshape(vregs * nb * MID, plan.tiles * LANES), untile[...])
    rows[ROWS:, :] = jnp.ones((ONES, 8 * LANES), BF)
    for n in range(nb):
        for v in range(8):
            lanes = slice(v * LANES, (v + 1) * LANES)
            w, at = v // per, v % per
            base = (w * nb + n) * MID
            here = g[base : base + MID, at * LANES : (at + 1) * LANES] * slope[n, :, lanes].astype(F32)
            here = here.astype(BF).astype(F32)
            cols[:MID, lanes] = shift_cols(here, 1, COARSE).astype(BF)
            cols[MID : 2 * MID, lanes] = here.astype(BF)
            cols[2 * MID : COLS, lanes] = shift_cols(here, -1, COARSE).astype(BF)
        q = dot(weights[...], cols[...])
        for pr in range(2):
            reg = {
                t: [q[t * MID : (t + 1) * MID, v * LANES : (v + 1) * LANES] for v in range(8)]
                for t in range(pr, TAPS, 2)
            }
            fine = up_rows(reg, pr, 2, 4, COARSE)
            for v in range(8):
                out = fine[v].astype(BF)
                for pc in range(2):
                    cut = slice((2 * pr + pc) * LANES, (2 * pr + pc + 1) * LANES)
                    lo[v, n, :, cut] = out[pc * FINE : (pc + 1) * FINE]
            source = [
                phases[n, pr * 2 * FINE : (pr + 1) * 2 * FINE, v * LANES : (v + 1) * LANES].astype(F32)
                for v in range(8)
            ]
            for t in range(pr, TAPS, 2):
                moved = source if t // 2 == 1 else shift_rows(source, tap_of(t)[1], 2, 4, COARSE)
                for v in range(8):
                    rows[t * MID : (t + 1) * MID, v * LANES : (v + 1) * LANES] = moved[v].astype(BF)
        total[:, :COLS] += dot_nt(rows[...], cols[...])
    nat = dot(lo[...].reshape(8 * nb * FINE, 512), join[...])
    for n in range(nb):
        keep = kept(counts[first + n])
        for i in range(COARSE):
            r, m, u = i // 16, i % 16 // 4, i % 4
            at = ((r * 4 + u) * nb + n) * FINE
            piece = jnp.where(keep, nat[at : at + FINE, m * LANES : (m + 1) * LANES], 0.0)
            grad[n, :, i * LANES : (i + 1) * LANES] = piece.astype(BF)

    @pl.when(step == pl.num_programs(0) - 1)
    def _():
        for t in range(TAPS):
            for s in range(TAPS):
                at = (2 * t + s % 2) * FINE
                tap = total[at : at + FINE, s // 4 * LANES : (s // 4 + 1) * LANES]
                if s // 2 == 1:
                    tap = turn(tap, MID)
                taps[TAPS * t + s] = tap.T[:MID]


def reduce_kernel(axes, enc, enc_bias, dec, dec_bias, *refs):
    outs, (packed, parts, full, far), sems = refs[:4], refs[4:8], refs[8:]
    n_ga, n_ty, n_tx = axes
    ga, ty, tx = lax.axis_index("ga"), lax.axis_index("ty"), lax.axis_index("tx")
    me, n = ga * n_ty + ty, n_ga * n_ty
    lanes = 2 * enc.shape[1] // n

    def near(d):
        to = (me + d) % n
        return to, {"ga": to // n_ty, "ty": to % n_ty}

    def along(d):
        return {"tx": (tx + d) % n_tx}

    def piece(ref, p):
        return ref.at[p // (n // 2), :, pl.ds(pl.multiple_of(p % (n // 2) * lanes, LANES), lanes)]

    barrier = pltpu.get_barrier_semaphore()
    for d in range(1, n):
        pl.semaphore_signal(barrier, inc=1, device_id=near(d)[1], device_id_type=pl.DeviceIdType.MESH)
    for d in range(1, n_tx):
        pl.semaphore_signal(barrier, inc=1, device_id=along(d), device_id_type=pl.DeviceIdType.MESH)
    packed[:, 24:] = jnp.zeros((2, 8, enc.shape[1]), F32)
    packed[0, :25] = enc[...]
    packed[1, :25] = dec[...]
    packed[0, 25:26, :LANES] = enc_bias[:1]
    packed[1, 25:26, :LANES] = dec_bias[...]
    pl.semaphore_wait(barrier, n - 1 + n_tx - 1)

    def exchange(peers, source, target, send, recv):
        copies = [
            pltpu.make_async_remote_copy(
                src_ref=source(d),
                dst_ref=target(d),
                send_sem=send.at[d],
                recv_sem=recv.at[d],
                device_id=to,
                device_id_type=pl.DeviceIdType.MESH,
            )
            for d, to in peers
        ]
        for copy in copies:
            copy.start()
        for copy in copies:
            copy.wait()

    plane = [(d, near(d)[1]) for d in range(1, n)]
    exchange(plane, lambda d: piece(packed, near(d)[0]), lambda d: parts.at[d], sems[0], sems[1])
    mine = piece(packed, me)[...]
    for d in range(1, n):
        mine = mine + parts[d]
    far[tx] = mine
    exchange([(d, along(d)) for d in range(1, n_tx)], lambda d: far.at[tx], lambda d: far.at[tx], sems[2], sems[3])
    mine = far[0]
    for t in range(1, n_tx):
        mine = mine + far[t]
    piece(full, me)[...] = mine
    exchange(plane, lambda d: piece(full, me), lambda d: piece(full, me), sems[4], sems[5])
    outs[0][...] = full[0, :25]
    outs[1][...] = full[1, :25]
    outs[2][...] = full[0, 25:26, :LANES]
    outs[3][...] = full[1, 25:26, :LANES]


def block(array):
    return pl.BlockSpec(array.shape, lambda *_: (0,) * array.ndim)


SMEM = pl.BlockSpec(memory_space=pltpu.SMEM)
ANYWHERE = pl.BlockSpec(memory_space=pl.ANY)


def params(steps):
    return pltpu.CompilerParams(dimension_semantics=("arbitrary",) * steps, vmem_limit_bytes=VMEM_BYTES)


def shape(dims, dtype=BF):
    return jax.ShapeDtypeStruct(dims, dtype)


def encode(plan, ns, chunk, size, nb, extra, place, counts, x, consts, own=None):
    per, skip, steps = 8 // plan.vregs, chunk // nb, size // nb
    packets = pl.BlockSpec((nb // 2, MID, plan.packet), lambda i, at: (i, 0, 0))
    carry, carried = [], []
    if own is not None:
        dims = (plan.tiles // steps, *own.shape[2:])
        carry = [pl.BlockSpec((1, *dims), lambda i, at: (1 - at[0], i, 0, 0, 0))]
        carried = [pl.BlockSpec((1, *dims), lambda i, at: (0, i, 0, 0, 0))]
    out = pl.pallas_call(
        functools.partial(encode_kernel, plan, ns, chunk, nb, len(carry)),
        grid_spec=pltpu.PrefetchScalarGridSpec(
            num_scalar_prefetch=1,
            grid=(steps,),
            in_specs=[SMEM, pl.BlockSpec((nb, FINE, GRID * GRID), lambda i, at: (skip + i, 0, 0))]
            + [block(a) for a in consts]
            + carry,
            out_specs=[packets] * plan.tiles
            + [
                pl.BlockSpec((nb, MID, 8 * LANES), lambda i, at: (i, 0, 0)),
                pl.BlockSpec((nb, 4 * FINE, 8 * LANES), lambda i, at: (i, 0, 0)),
                SMEM,
            ]
            + carried,
            scratch_shapes=[
                pltpu.VMEM((8, nb, FINE, 512), BF),
                pltpu.VMEM((ROWS, 8 * LANES), BF),
                pltpu.VMEM((plan.vregs, nb, MID, per * LANES), BF),
                pltpu.VMEM((plan.tiles, nb // 2, MID, 2 * plan.vregs * LANES), BF),
                pltpu.VMEM((plan.tiles, nb // 2, MID, plan.packet), BF),
            ],
        ),
        out_shape=[shape((size // 2 + (extra if k else 0), MID, plan.packet)) for k in range(plan.tiles)]
        + [shape((size, MID, 8 * LANES)), shape((size, 4 * FINE, 8 * LANES)), shape((2,), jnp.int32)]
        + [shape((1, *own.shape[1:])) for _ in carry],
        compiler_params=params(1),
        name=f"encode{size}",
    )(place, counts, x, *consts, *([own] if carry else []))
    return out[: plan.tiles], *out[plan.tiles :]


def decode(plan, ns, chunk, size, nb, place, got, counts, own, other, before, consts, home, away, span, bufs, offset):
    skip, steps = chunk // nb, size // nb
    lanes = nb * plan.vregs * LANES
    flat = GRID * plan.width
    picture = pl.BlockSpec((1, 1, nb, FINE, flat), lambda s, i, at: (at[0], at[1] ^ s, skip + i, 0, 0))

    def packets(k, off):
        return pl.BlockSpec(
            (nb // 2, MID, plan.packet),
            lambda s, i, at: (off // (nb // 2) + jnp.where(s == k, i, jnp.where(s < k, 0, steps - 1)), 0, 0),
        )

    args = (*got, counts, own, other, before) + consts
    specs = (
        [packets(k, 0) for k in range(plan.tiles)]
        + [SMEM, picture, pl.BlockSpec((1, nb, FINE, flat), lambda s, i, at: (at[1] ^ s, skip + i, 0, 0)), block(before)]
        + [block(a) for a in consts]
    )
    alias = {}
    for to, array in enumerate((home, away, None, None, *(bufs or ()))):
        if array is not None:
            alias[len(args) + 1] = to
            args, specs = args + (array,), specs + [ANYWHERE]
    home, away, total, *send = pl.pallas_call(
        functools.partial(decode_kernel, plan, ns, chunk, nb, len(alias)),
        grid_spec=pltpu.PrefetchScalarGridSpec(
            num_scalar_prefetch=1,
            grid=(plan.tiles, steps),
            in_specs=specs,
            out_specs=[
                picture,
                pl.BlockSpec((1, nb, FINE, flat), lambda s, i, at: (at[1] ^ s, skip - span[0] // nb + i, 0, 0)),
                block(before),
                *[packets(k, offset if k else 0) for k in range(plan.tiles)],
            ],
            scratch_shapes=[
                pltpu.VMEM((plan.vregs, nb, FINE, 512), BF),
                pltpu.VMEM((COLS + ONES, lanes), BF),
                pltpu.VMEM((ROWS, lanes), BF),
                pltpu.VMEM((plan.vregs, nb, FINE, 512), BF),
                pltpu.VMEM((nb // 2, MID, 2 * plan.vregs * LANES), BF),
                pltpu.VMEM((nb // 2, MID, plan.packet), BF),
                pltpu.VMEM((nb // 2, MID, plan.packet), BF),
            ],
        ),
        out_shape=[
            shape(own.shape),
            shape((plan.tiles, span[1] - span[0], FINE, flat)),
            shape(before.shape, F32),
            shape((size // 2, MID, plan.packet)),
            *[shape(b.shape if bufs else (size // 2, MID, plan.packet)) for b in (bufs or got[1:])],
        ],
        input_output_aliases=alias,
        compiler_params=params(2),
        name=f"decode{size}",
    )(place, *args)
    return home, away, total, send


def back(plan, ns, chunk, size, nb, place, counts, got, offset, slope, phases, before, consts, grad):
    skip = chunk // nb
    per = 8 // plan.vregs
    args = (counts, *got, slope, phases, before) + consts
    specs = (
        [SMEM]
        + [
            pl.BlockSpec((nb // 2, MID, plan.packet), lambda i, at, off=off: (off // (nb // 2) + i, 0, 0))
            for off in [0] + [offset] * (plan.tiles - 1)
        ]
        + [
            pl.BlockSpec((nb, MID, 8 * LANES), lambda i, at: (i, 0, 0)),
            pl.BlockSpec((nb, 4 * FINE, 8 * LANES), lambda i, at: (i, 0, 0)),
            block(before),
        ]
        + [block(a) for a in consts]
    )
    alias = {}
    if grad is not None:
        alias[len(args) + 1] = 0
        args, specs = args + (grad,), specs + [ANYWHERE]
    return pl.pallas_call(
        functools.partial(back_kernel, plan, ns, chunk, nb, int(grad is not None)),
        grid_spec=pltpu.PrefetchScalarGridSpec(
            num_scalar_prefetch=1,
            grid=(size // nb,),
            in_specs=specs,
            out_specs=[
                pl.BlockSpec((nb, FINE, GRID * GRID), lambda i, at: (skip + i, 0, 0)),
                block(before),
                pl.BlockSpec((TAPS * TAPS, MID, FINE), lambda i, at: (0, 0, 0)),
            ],
            scratch_shapes=[
                pltpu.VMEM((plan.tiles, nb // 2, MID, plan.packet), BF),
                pltpu.VMEM((plan.vregs, nb, MID, plan.tiles * LANES), BF),
                pltpu.VMEM((COLS, 8 * LANES), BF),
                pltpu.VMEM((ROWS + ONES, 8 * LANES), BF),
                pltpu.VMEM((8, nb, FINE, 512), BF),
            ],
        ),
        out_shape=[
            shape((ns, FINE, GRID * GRID)),
            shape(before.shape, F32),
            shape((TAPS * TAPS, MID, FINE), F32),
        ],
        input_output_aliases=alias,
        compiler_params=params(1),
        name=f"back{size}",
    )(place, *args)


def reduce(enc, enc_total, dec, dec_bias):
    axes = tuple(lax.axis_size(name) for name in ("ga", "ty", "tx"))
    n = axes[0] * axes[1]
    size = enc.shape[1]
    piece = (32, 2 * size // n)
    sems = [pltpu.SemaphoreType.DMA((n,))] * 2 + [pltpu.SemaphoreType.DMA((axes[2],))] * 2
    return pl.pallas_call(
        functools.partial(reduce_kernel, axes),
        grid=(1,),
        in_specs=[block(enc), pl.BlockSpec((8, LANES), lambda i: (ROWS // 8, 0)), block(dec), block(dec_bias)],
        out_specs=[block(enc), block(dec), block(dec_bias), block(dec_bias)],
        out_shape=[shape(enc.shape, F32), shape(dec.shape, F32), *[shape(dec_bias.shape, F32)] * 2],
        scratch_shapes=[
            pltpu.VMEM((2, 32, size), F32),
            pltpu.VMEM((n, *piece), F32),
            pltpu.VMEM((2, 32, size), F32),
            pltpu.VMEM((axes[2], *piece), F32),
            *sems,
            *sems[:2],
        ],
        compiler_params=pltpu.CompilerParams(collective_id=0, has_side_effects=True, vmem_limit_bytes=VMEM_BYTES),
        name="reduce",
    )(enc, enc_total, dec, dec_bias)


def kernel_matrix(kernel):
    spread = jnp.pad(kernel, ((0, 0), (0, 1), (0, 0), (0, 0))).reshape(TAPS, 3, 2, FINE, MID)
    return spread.transpose(0, 2, 3, 1, 4).reshape(ROWS, COLS)


def taps_of(total):
    split = total[:, :COLS].reshape(TAPS, 2, FINE, 3, MID).transpose(0, 3, 1, 2, 4)
    return split.reshape(TAPS, 6, FINE, MID)[:, :TAPS]


def body(snapshots, counts, enc_weight, enc_bias, dec_weight, dec_bias, cotangent):
    ns = snapshots.shape[0]
    sides, tiles = lax.axis_size("ty"), lax.axis_size("tx")
    plan = Plan(tiles)
    half = tiles * ns
    ty, tx = lax.axis_index("ty"), lax.axis_index("tx")
    half_counts = lax.dynamic_slice_in_dim(counts, ty * half, half)
    sizes = [8, 16, 16, 8] if ns == 48 else [4] * (ns // 4)
    starts = [sum(sizes[:c]) for c in range(len(sizes))]
    chunks = len(sizes)
    nb = 4
    place = jnp.stack([ty, tx]).astype(jnp.int32)

    def swapped(array, axis, k):
        size = lax.axis_size(axis)
        return array if k == 0 else lax.ppermute(array, axis, [(i, i ^ k) for i in range(size)])

    split, image_join = jnp.asarray(image_split()), jnp.asarray(image_split().T)
    cot_split, cot_join = jnp.asarray(tile_split(plan)), jnp.asarray(tile_split(plan).T)
    into, out_of = jnp.asarray(to_tiles(plan)), jnp.asarray(to_tiles(plan).T)
    edges = jnp.asarray(edge_pick(plan, 0))
    spread = jnp.asarray(edge_pick(plan, 1).T)
    shifts = jnp.asarray(column_shifts(plan))
    enc = kernel_matrix(enc_weight.transpose(2, 3, 1, 0))
    dec = kernel_matrix(dec_weight.transpose(2, 3, 0, 1)[::-1, ::-1])
    enc_b = jnp.broadcast_to(enc_bias.astype(F32)[:, None], (MID, LANES))
    dec_b = jnp.broadcast_to(jnp.tile(dec_bias.astype(F32), 2)[:, None], (MID, LANES))

    enc_consts = (split, into, edges, enc.T, enc_b)
    dec_consts = (cot_split, cot_join, shifts, edges, dec, dec.T, dec_b)
    back_consts = (spread, out_of, image_join, enc)

    def pairs(c):
        return sizes[c] // 2 if 0 <= c < chunks else 0

    def run_encode(c, there, own=None):
        return encode(plan, ns, starts[c], sizes[c], nb, pairs(c - 2), there, counts, snapshots, enc_consts, own)

    own = cotangent.reshape(sides, tiles, ns, FINE, -1)
    spans = ((0, starts[-1]), (starts[-1], ns))
    home, away, arrived = None, [None, None], [None, None]
    dec_total = jnp.zeros((ROWS, 2 * LANES), F32)
    enc_total = jnp.zeros((ROWS + ONES, 2 * LANES), F32)
    grad, got, other, lent, dec_flat = None, None, None, None, None
    fronts, extras, backs = {}, {}, {}
    (fronts[0], *bufs), *extras[0], there = run_encode(0, place)
    for s in range(chunks + 3):
        sent = [swapped(buf, "tx", k) for k, buf in enumerate(bufs, 1)] if bufs else None
        bufs = None
        if s == 1:
            other = swapped(lent, "ty", 1)
        if 0 <= s - chunks < 2:
            arrived[s - chunks] = swapped(away[s - chunks], "ty", 1)
        if s + 1 < chunks:
            (fronts[s + 1], *bufs), *extras[s + 1], there = run_encode(s + 1, there, None if s else own)
            if s == 0:
                there, lent = extras[1].pop(), there[0]
        if 0 <= s - 1 < chunks:
            c = s - 1
            late = int(c == chunks - 1)
            home, away[late], dec_total, (backs[c], *bufs) = decode(
                plan,
                ns,
                starts[c],
                sizes[c],
                4 if sizes[c] % 8 else 8,
                place,
                [fronts[c], *got],
                half_counts,
                own,
                other,
                dec_total,
                dec_consts,
                home,
                away[late],
                spans[late],
                bufs,
                pairs(s + 1),
            )
        if s - 3 >= 0:
            c = s - 3
            grad, enc_total, enc_taps = back(
                plan,
                ns,
                starts[c],
                sizes[c],
                nb,
                place,
                counts,
                [backs[c], *got],
                pairs(s - 1),
                *extras[c],
                enc_total,
                back_consts,
                grad,
            )
        if s == chunks:
            dec_taps = taps_of(dec_total)[::-1, ::-1].reshape(25, FINE * MID)
            dec_bias_part = dec_total[2 * MID : 4 * MID, COLS].reshape(4, FINE).sum(0)
            dec_bias_part = jnp.pad(dec_bias_part[None], ((0, 0), (0, LANES - FINE)))
            dec_flat = (dec_taps, dec_bias_part)
        for late in range(2):
            if s == chunks + 1 + late:
                home = lax.dynamic_update_slice(home, arrived[late][None], (1 - ty, 0, spans[late][0], 0, 0))
        if s < chunks + 2:
            state = (sent, bufs, fronts, home, away, arrived, dec_total, grad, enc_total, dec_flat, there, lent)
            state = lax.optimization_barrier(state)
            got, bufs, fronts, home, away, arrived, dec_total, grad, enc_total, dec_flat, there, lent = state
    enc_weight_grad, dec_weight_grad, enc_bias_grad, dec_bias_grad = reduce(
        enc_taps.reshape(25, MID * FINE), enc_total, *dec_flat
    )
    enc_bias_grad, dec_bias_grad = enc_bias_grad[0, MID:], dec_bias_grad[0, :FINE]
    decoded = home.reshape(cotangent.shape)
    return (decoded, grad, enc_weight_grad, enc_bias_grad, dec_weight_grad, dec_bias_grad)


def solution(mesh):
    return jax.shard_map(
        body,
        mesh=mesh,
        in_specs=(
            P(("ga", "ty", "tx"), None, None),
            P("ga"),
            P(),
            P(),
            P(),
            P(),
            P("ga", None, "ty", "tx", None),
        ),
        out_specs=(
            P("ga", None, "ty", "tx", None),
            P(("ga", "ty", "tx"), None, None),
            P(),
            P(),
            P(),
            P(),
        ),
        check_vma=False,
    )
```

```python
import functools

import jax
import jax.numpy as jnp
import ml_dtypes
import numpy as np
from jax import lax
from jax.experimental import pallas as pl
from jax.experimental.pallas import tpu as pltpu
from jax.sharding import PartitionSpec as P


FINE = 32
MID = 64
GRID = 64
COARSE = 32
LANES = 128
TAPS = 5
ROWS = TAPS * 2 * FINE
COLS = 3 * MID
ONES = 16
UNIT = 4
BF = jnp.bfloat16
F32 = jnp.float32
VMEM_BYTES = 56 * 1024 * 1024


class Plan:
    def __init__(self, tiles):
        self.tiles = tiles
        self.width = COARSE // tiles
        self.vregs = COARSE * self.width // LANES
        self.rows = LANES // self.width
        self.packet = 2 * self.vregs * LANES + LANES


def one(matrix):
    return matrix.astype(ml_dtypes.bfloat16)


def image_split():
    out = np.zeros((4, 2, 32, 2, 2, 2, 4, 32), np.float32)
    for m in range(4):
        for pr in range(2):
            for j in range(32):
                for pc in range(2):
                    out[m, pr, j, pc, pr, pc, m, j] = 1
    return one(out.reshape(512, 512))


def tile_split(plan):
    n, w = plan.rows, plan.width
    out = np.zeros((n, 2, w, 2, 2, 2, n, w), np.float32)
    for i in range(n):
        for pr in range(2):
            for j in range(w):
                for pc in range(2):
                    out[i, pr, j, pc, pr, pc, i, j] = 1
    return one(out.reshape(512, 512))


def to_tiles(plan):
    halves = 2 // plan.vregs
    out = np.zeros((halves, 4, 4, plan.tiles, plan.width, plan.tiles, halves, 4, 4, plan.width), np.float32)
    for r in range(halves):
        for u in range(4):
            for m in range(4):
                for t in range(plan.tiles):
                    for j in range(plan.width):
                        out[r, u, m, t, j, t, r, m, u, j] = 1
    size = halves * 4 * LANES
    return one(out.reshape(size, size))


def edge_pick(plan, swap):
    v, n, w = plan.vregs, plan.rows, plan.width
    out = np.zeros((2, v, n, w, 2, v, 2, n), np.float32)
    for p in range(2):
        for q in range(v):
            for i in range(n):
                for edge in range(2):
                    out[p, q, i, (w - 1) * (edge ^ swap), p, q, edge, i] = 1
    return one(out.reshape(2 * v * LANES, LANES))


def column_shifts(plan):
    v, n, w = plan.vregs, plan.rows, plan.width
    out = np.zeros((2, v, 2, LANES, 2, n, w), np.float32)
    for p in range(2):
        for q in range(v):
            for i in range(n):
                for j in range(w):
                    if j < w - 1:
                        out[p, q, 0, i * w + j + 1, 0, i, j] = 1
                    else:
                        out[p, q, 1, ((p * v + q) * 2 + 0) * n + i, 0, i, j] = 1
                    if j > 0:
                        out[p, q, 0, i * w + j - 1, 1, i, j] = 1
                    else:
                        out[p, q, 1, ((p * v + q) * 2 + 1) * n + i, 1, i, j] = 1
    return one(out.reshape(2 * v, 2 * LANES, 2 * LANES))


def dot(a, b):
    return jnp.dot(a, b, preferred_element_type=F32)


def dot_nt(a, b):
    return lax.dot_general(a, b, (((1,), (1,)), ((), ())), preferred_element_type=F32)


def lane_of(rows):
    return lax.broadcasted_iota(jnp.int32, (rows, LANES), 1)


def turn(x, by):
    return pltpu.roll(x, (-by) % LANES, 1)


def shift_rows(pieces, d, halves, inner, step):
    lane = lane_of(pieces[0].shape[0])
    out = []
    for r in range(halves):
        for u in range(inner):
            if 0 <= u + d < inner:
                out.append(pieces[r * inner + u + d])
            elif d > 0:
                here = turn(pieces[r * inner], step)
                after = turn(pieces[(r + 1) * inner], step) if r + 1 < halves else 0.0
                out.append(jnp.where(lane < LANES - step, here, after))
            else:
                here = turn(pieces[r * inner + inner - 1], -step)
                before = turn(pieces[r * inner - 1], -step) if r else 0.0
                out.append(jnp.where(lane >= step, here, before))
    return out


def shift_cols(x, d, width):
    j = lane_of(x.shape[0]) & (width - 1)
    return jnp.where(j < width - 1 if d > 0 else j >= 1, turn(x, d), 0.0)


def tap_of(t):
    return t % 2, t // 2 - 1


def up_rows(q, parity, halves, inner, step):
    total = None
    for t in range(parity, TAPS, 2):
        d = -tap_of(t)[1]
        part = q[t] if d == 0 else shift_rows(q[t], d, halves, inner, step)
        total = part if total is None else [a + b for a, b in zip(total, part)]
    return total


def kept(count):
    return lax.broadcasted_iota(jnp.int32, (FINE, LANES), 0) // (FINE // 4) < count


def encode_kernel(plan, ns, chunk, nb, carried, place, counts, x, split, tiles, edges, weights_t, bias, *rest):
    refs, rest = rest[:carried], rest[carried:]
    send, (slope, phases, there, *rest) = rest[: plan.tiles], rest[plan.tiles :]
    refs, (lx, rows, lt, lc, stage) = (*refs, *rest[:carried]), rest[carried:]
    there[0], there[1] = place[0], place[1]
    first = (place[0] * plan.tiles + place[1]) * ns + chunk + pl.program_id(0) * nb
    tx = place[1]
    width, vregs, per = plan.width, plan.vregs, 8 // plan.vregs
    if carried:
        refs[-1][...] = refs[-2][...]
    for n in range(nb):
        keep = kept(counts[first + n]).astype(BF)
        for i in range(COARSE):
            r, m, u = i // 16, i % 16 // 4, i % 4
            lx[r * 4 + u, n, :, m * LANES : (m + 1) * LANES] = x[n, :, i * LANES : (i + 1) * LANES] * keep
    y = dot(lx[...].reshape(8 * nb * FINE, 512), split[...])
    for n in range(nb):
        for ph in range(4):
            pr, pc = ph // 2, ph % 2
            pieces = [
                y[(v * nb + n) * FINE : (v * nb + n + 1) * FINE, ph * LANES : (ph + 1) * LANES] for v in range(8)
            ]
            for v in range(8):
                phases[n, ph * FINE : (ph + 1) * FINE, v * LANES : (v + 1) * LANES] = pieces[v].astype(BF)
            for t in range(pr, TAPS, 2):
                d = tap_of(t)[1]
                moved = shift_rows(pieces, d, 2, 4, COARSE)
                at = (t * 2 + pc) * FINE
                for v in range(8):
                    rows[at : at + FINE, v * LANES : (v + 1) * LANES] = moved[v].astype(BF)
        s = dot(weights_t[...], rows[...])
        for v in range(8):
            cut = slice(v * LANES, (v + 1) * LANES)
            pre = s[MID : 2 * MID, cut] + bias[...]
            pre += shift_cols(s[:MID, cut], -1, COARSE) + shift_cols(s[2 * MID :, cut], 1, COARSE)
            e = jnp.exp(jnp.minimum(pre, 0.0))
            slope[n, :, cut] = e.astype(BF)
            hidden = jnp.where(pre > 0, pre, e - 1.0).astype(BF)
            w, at = v // per, v % per
            lt[w, n, :, at * LANES : (at + 1) * LANES] = hidden
    z = dot(lt[...].reshape(vregs * nb * MID, per * LANES), tiles[...])
    j = lane_of(MID) & (width - 1)
    for n in range(nb):
        for w in range(vregs):
            at = (w * nb + n) * MID
            main = [z[at : at + MID, t * LANES : (t + 1) * LANES] for t in range(plan.tiles)]
            cut = slice((n % 2 * vregs + w) * LANES, (n % 2 * vregs + w + 1) * LANES)
            for t in range(plan.tiles):
                stage[t, n // 2, :, cut] = main[t].astype(BF)
                left = main[t - 1] if t else 0.0
                right = main[t + 1] if t + 1 < plan.tiles else 0.0
                rim = jnp.where(j == 0, right, jnp.where(j == width - 1, left, 0.0))
                lc[t, n // 2, :, cut] = rim.astype(BF)
    rims = dot(lc[...].reshape(plan.tiles * nb // 2 * MID, 2 * vregs * LANES), edges[...])
    for t in range(plan.tiles):
        for pair in range(nb // 2):
            at = (t * nb // 2 + pair) * MID
            stage[t, pair, :, 2 * vregs * LANES :] = rims[at : at + MID].astype(BF)
    for k in range(plan.tiles):
        send[k][...] = stage[tx ^ k]


def decode_kernel(plan, ns, chunk, nb, chained, place, *refs):
    parts, refs = refs[: plan.tiles], refs[plan.tiles :]
    counts, own, other, before, split, join, shifts, edges, weights, weights_t, bias = refs[:11]
    home, away, total, *refs = refs[11 + chained :]
    sends, (lcot, cols, rows, ldec, lc, got, send) = refs[: plan.tiles], refs[plan.tiles :]
    ty, part, step = place[0], pl.program_id(0), pl.program_id(1)
    upper = ty == 0
    first = (place[1] ^ part) * ns + chunk + step * nb
    width, vregs = plan.width, plan.vregs
    edge_at = 2 * vregs * LANES
    masks = [kept(counts[first + n]) for n in range(nb)]

    @pl.when((part == 0) & (step == 0))
    def _():
        total[...] = before[...]

    for k in range(plan.tiles):

        @pl.when(part == k)
        def _():
            got[...] = parts[k][...]

    half = 2 // vregs
    span = 4 // half
    for n in range(nb):
        keep = masks[n].astype(BF)
        for k in range(span):
            cut = slice(k * LANES, (k + 1) * LANES)
            mine, theirs = own[0, 0, n, :, cut] * keep, other[0, n, :, cut] * keep
            for side in range(2):
                k_to = k + side % half * span
                lcot[side // half, n, :, k_to * LANES : (k_to + 1) * LANES] = (
                    jnp.where(upper, mine, theirs) if side == 0 else jnp.where(upper, theirs, mine)
                )
    c = dot(lcot[...].reshape(vregs * nb * FINE, 512), split[...])
    for p in range(2):
        for w in range(vregs):
            slot = p * vregs + w
            at = slice(slot * LANES, (slot + 1) * LANES)
            both = jnp.concatenate([got[:, :, at], got[:, :, edge_at:]], axis=2)
            moved = dot(both.reshape(nb // 2 * MID, 2 * LANES), shifts[slot]).astype(BF)
            for pair in range(nb // 2):
                lanes = slice(((2 * pair + p) * vregs + w) * LANES, ((2 * pair + p) * vregs + w + 1) * LANES)
                sub = slice(pair * MID, (pair + 1) * MID)
                cols[:MID, lanes] = moved[sub, :LANES]
                cols[MID : 2 * MID, lanes] = got[pair, :, at]
                cols[2 * MID : COLS, lanes] = moved[sub, LANES:]
    cols[COLS:, :] = jnp.ones((ONES, nb * vregs * LANES), BF)
    q = dot(weights[...], cols[:COLS, :])
    for n in range(nb):
        for pr in range(2):
            reg = {
                t: [
                    q[t * MID : (t + 1) * MID, (n * vregs + w) * LANES : (n * vregs + w + 1) * LANES]
                    for w in range(vregs)
                ]
                for t in range(pr, TAPS, 2)
            }
            pre = [x + bias[...] for x in up_rows(reg, pr, vregs, 1, width)]
            grads = []
            for w in range(vregs):
                e = jnp.exp(jnp.minimum(pre[w], 0.0))
                at = (w * nb + n) * FINE
                tangent = jnp.concatenate(
                    [
                        c[at : at + FINE, (2 * pr + pc) * LANES : (2 * pr + pc + 1) * LANES]
                        for pc in range(2)
                    ],
                    axis=0,
                )
                grads.append(tangent * e)
                out = jnp.where(pre[w] > 0, pre[w], e - 1.0).astype(BF)
                for pc in range(2):
                    cut = slice((2 * pr + pc) * LANES, (2 * pr + pc + 1) * LANES)
                    ldec[w, n, :, cut] = out[pc * FINE : (pc + 1) * FINE]
            for t in range(pr, TAPS, 2):
                moved = grads if t // 2 == 1 else shift_rows(grads, tap_of(t)[1], vregs, 1, width)
                for w in range(vregs):
                    lanes = slice((n * vregs + w) * LANES, (n * vregs + w + 1) * LANES)
                    rows[t * MID : (t + 1) * MID, lanes] = moved[w].astype(BF)
    nat = dot(ldec[...].reshape(vregs * nb * FINE, 512), join[...])
    for n in range(nb):
        for k in range(span):
            sides = []
            for side in range(2):
                at = (side // half * nb + n) * FINE
                k_from = k + side % half * span
                sides.append(jnp.where(masks[n], nat[at : at + FINE, k_from * LANES : (k_from + 1) * LANES], 0.0))
            cut = slice(k * LANES, (k + 1) * LANES)
            home[0, 0, n, :, cut] = jnp.where(upper, sides[0], sides[1]).astype(BF)
            away[0, n, :, cut] = jnp.where(upper, sides[1], sides[0]).astype(BF)
    s = dot(weights_t[...], rows[...])
    j = lane_of(MID) & (width - 1)
    for n in range(nb):
        for w in range(vregs):
            lanes = slice((n * vregs + w) * LANES, (n * vregs + w + 1) * LANES)
            behind, here, ahead = s[:MID, lanes], s[MID : 2 * MID, lanes], s[2 * MID :, lanes]
            grad = here + shift_cols(behind, -1, width) + shift_cols(ahead, 1, width)
            slot = n % 2 * vregs + w
            cut = slice(slot * LANES, (slot + 1) * LANES)
            send[n // 2, :, cut] = grad.astype(BF)
            lc[n // 2, :, cut] = jnp.where(j == 0, ahead, behind).astype(BF)
    rims = dot(lc[...].reshape(nb // 2 * MID, edge_at), edges[...])
    for pair in range(nb // 2):
        send[pair, :, edge_at:] = rims[pair * MID : (pair + 1) * MID].astype(BF)
    total[:, : COLS + ONES] += dot_nt(rows[...], cols[...])
    for k in range(plan.tiles):

        @pl.when(part == k)
        def _():
            sends[k][...] = send[...]


def back_kernel(plan, ns, chunk, nb, chained, place, counts, *refs):
    parts, refs = refs[: plan.tiles], refs[plan.tiles :]
    slope, phases, before, spread, untile, join, weights = refs[:7]
    grad, total, taps, got, lu, cols, rows, lo = refs[7 + chained :]
    step = pl.program_id(0)
    first = (place[0] * plan.tiles + place[1]) * ns + chunk + step * nb
    tx = place[1]
    width, vregs, per = plan.width, plan.vregs, 8 // plan.vregs
    edge_at = 2 * vregs * LANES

    @pl.when(step == 0)
    def _():
        total[...] = before[...]

    for k in range(plan.tiles):
        got[tx ^ k] = parts[k][...]
    rims = dot(got[:, :, :, edge_at:].reshape(plan.tiles * nb // 2 * MID, LANES), spread[...])
    j = lane_of(MID) & (width - 1)
    for n in range(nb):
        for w in range(vregs):
            slot = n % 2 * vregs + w
            cut = slice(slot * LANES, (slot + 1) * LANES)
            rim = [
                rims[(t * nb // 2 + n // 2) * MID : (t * nb // 2 + n // 2 + 1) * MID, cut] for t in range(plan.tiles)
            ]
            for t in range(plan.tiles):
                main = got[t, n // 2, :, cut].astype(F32)
                if t + 1 < plan.tiles:
                    main += jnp.where(j == width - 1, rim[t + 1], 0.0)
                if t:
                    main += jnp.where(j == 0, rim[t - 1], 0.0)
                lu[w, n, :, t * LANES : (t + 1) * LANES] = main.astype(BF)
    g = dot(lu[...].reshape(vregs * nb * MID, plan.tiles * LANES), untile[...])
    rows[ROWS:, :] = jnp.ones((ONES, 8 * LANES), BF)
    for n in range(nb):
        for v in range(8):
            lanes = slice(v * LANES, (v + 1) * LANES)
            w, at = v // per, v % per
            base = (w * nb + n) * MID
            here = g[base : base + MID, at * LANES : (at + 1) * LANES] * slope[n, :, lanes].astype(F32)
            here = here.astype(BF).astype(F32)
            cols[:MID, lanes] = shift_cols(here, 1, COARSE).astype(BF)
            cols[MID : 2 * MID, lanes] = here.astype(BF)
            cols[2 * MID : COLS, lanes] = shift_cols(here, -1, COARSE).astype(BF)
        q = dot(weights[...], cols[...])
        for pr in range(2):
            reg = {
                t: [q[t * MID : (t + 1) * MID, v * LANES : (v + 1) * LANES] for v in range(8)]
                for t in range(pr, TAPS, 2)
            }
            fine = up_rows(reg, pr, 2, 4, COARSE)
            for v in range(8):
                out = fine[v].astype(BF)
                for pc in range(2):
                    cut = slice((2 * pr + pc) * LANES, (2 * pr + pc + 1) * LANES)
                    lo[v, n, :, cut] = out[pc * FINE : (pc + 1) * FINE]
            source = [
                phases[n, pr * 2 * FINE : (pr + 1) * 2 * FINE, v * LANES : (v + 1) * LANES].astype(F32)
                for v in range(8)
            ]
            for t in range(pr, TAPS, 2):
                moved = source if t // 2 == 1 else shift_rows(source, tap_of(t)[1], 2, 4, COARSE)
                for v in range(8):
                    rows[t * MID : (t + 1) * MID, v * LANES : (v + 1) * LANES] = moved[v].astype(BF)
        total[:, :COLS] += dot_nt(rows[...], cols[...])
    nat = dot(lo[...].reshape(8 * nb * FINE, 512), join[...])
    for n in range(nb):
        keep = kept(counts[first + n])
        for i in range(COARSE):
            r, m, u = i // 16, i % 16 // 4, i % 4
            at = ((r * 4 + u) * nb + n) * FINE
            piece = jnp.where(keep, nat[at : at + FINE, m * LANES : (m + 1) * LANES], 0.0)
            grad[n, :, i * LANES : (i + 1) * LANES] = piece.astype(BF)

    @pl.when(step == pl.num_programs(0) - 1)
    def _():
        for t in range(TAPS):
            for s in range(TAPS):
                at = (2 * t + s % 2) * FINE
                tap = total[at : at + FINE, s // 4 * LANES : (s // 4 + 1) * LANES]
                if s // 2 == 1:
                    tap = turn(tap, MID)
                taps[TAPS * t + s] = tap.T[:MID]


def reduce_kernel(axes, enc, enc_bias, dec, dec_bias, *refs):
    outs, (packed, parts, full, far), sems = refs[:4], refs[4:8], refs[8:]
    n_ga, n_ty, n_tx = axes
    ga, ty, tx = lax.axis_index("ga"), lax.axis_index("ty"), lax.axis_index("tx")
    me, n = ga * n_ty + ty, n_ga * n_ty
    lanes = 2 * enc.shape[1] // n

    def near(d):
        to = (me + d) % n
        return to, {"ga": to // n_ty, "ty": to % n_ty}

    def along(d):
        return {"tx": (tx + d) % n_tx}

    def piece(ref, p):
        return ref.at[p // (n // 2), :, pl.ds(pl.multiple_of(p % (n // 2) * lanes, LANES), lanes)]

    barrier = pltpu.get_barrier_semaphore()
    for d in range(1, n):
        pl.semaphore_signal(barrier, inc=1, device_id=near(d)[1], device_id_type=pl.DeviceIdType.MESH)
    for d in range(1, n_tx):
        pl.semaphore_signal(barrier, inc=1, device_id=along(d), device_id_type=pl.DeviceIdType.MESH)
    packed[:, 24:] = jnp.zeros((2, 8, enc.shape[1]), F32)
    packed[0, :25] = enc[...]
    packed[1, :25] = dec[...]
    packed[0, 25:26, :LANES] = enc_bias[:1]
    packed[1, 25:26, :LANES] = dec_bias[...]
    pl.semaphore_wait(barrier, n - 1 + n_tx - 1)

    def exchange(peers, source, target, send, recv):
        copies = [
            pltpu.make_async_remote_copy(
                src_ref=source(d),
                dst_ref=target(d),
                send_sem=send.at[d],
                recv_sem=recv.at[d],
                device_id=to,
                device_id_type=pl.DeviceIdType.MESH,
            )
            for d, to in peers
        ]
        for copy in copies:
            copy.start()
        for copy in copies:
            copy.wait()

    plane = [(d, near(d)[1]) for d in range(1, n)]
    exchange(plane, lambda d: piece(packed, near(d)[0]), lambda d: parts.at[d], sems[0], sems[1])
    mine = piece(packed, me)[...]
    for d in range(1, n):
        mine = mine + parts[d]
    far[tx] = mine
    exchange([(d, along(d)) for d in range(1, n_tx)], lambda d: far.at[tx], lambda d: far.at[tx], sems[2], sems[3])
    mine = far[0]
    for t in range(1, n_tx):
        mine = mine + far[t]
    piece(full, me)[...] = mine
    exchange(plane, lambda d: piece(full, me), lambda d: piece(full, me), sems[4], sems[5])
    outs[0][...] = full[0, :25]
    outs[1][...] = full[1, :25]
    outs[2][...] = full[0, 25:26, :LANES]
    outs[3][...] = full[1, 25:26, :LANES]


def block(array):
    return pl.BlockSpec(array.shape, lambda *_: (0,) * array.ndim)


SMEM = pl.BlockSpec(memory_space=pltpu.SMEM)
ANYWHERE = pl.BlockSpec(memory_space=pl.ANY)


def params(steps):
    return pltpu.CompilerParams(dimension_semantics=("arbitrary",) * steps, vmem_limit_bytes=VMEM_BYTES)


def shape(dims, dtype=BF):
    return jax.ShapeDtypeStruct(dims, dtype)


def encode(plan, ns, chunk, size, nb, extra, place, counts, x, consts, own=None):
    per, skip, steps = 8 // plan.vregs, chunk // nb, size // nb
    packets = pl.BlockSpec((nb // 2, MID, plan.packet), lambda i, at: (i, 0, 0))
    carry, carried = [], []
    if own is not None:
        dims = (plan.tiles // steps, *own.shape[2:])
        carry = [pl.BlockSpec((1, *dims), lambda i, at: (1 - at[0], i, 0, 0, 0))]
        carried = [pl.BlockSpec((1, *dims), lambda i, at: (0, i, 0, 0, 0))]
    out = pl.pallas_call(
        functools.partial(encode_kernel, plan, ns, chunk, nb, len(carry)),
        grid_spec=pltpu.PrefetchScalarGridSpec(
            num_scalar_prefetch=1,
            grid=(steps,),
            in_specs=[SMEM, pl.BlockSpec((nb, FINE, GRID * GRID), lambda i, at: (skip + i, 0, 0))]
            + [block(a) for a in consts]
            + carry,
            out_specs=[packets] * plan.tiles
            + [
                pl.BlockSpec((nb, MID, 8 * LANES), lambda i, at: (i, 0, 0)),
                pl.BlockSpec((nb, 4 * FINE, 8 * LANES), lambda i, at: (i, 0, 0)),
                SMEM,
            ]
            + carried,
            scratch_shapes=[
                pltpu.VMEM((8, nb, FINE, 512), BF),
                pltpu.VMEM((ROWS, 8 * LANES), BF),
                pltpu.VMEM((plan.vregs, nb, MID, per * LANES), BF),
                pltpu.VMEM((plan.tiles, nb // 2, MID, 2 * plan.vregs * LANES), BF),
                pltpu.VMEM((plan.tiles, nb // 2, MID, plan.packet), BF),
            ],
        ),
        out_shape=[shape((size // 2 + (extra if k else 0), MID, plan.packet)) for k in range(plan.tiles)]
        + [shape((size, MID, 8 * LANES)), shape((size, 4 * FINE, 8 * LANES)), shape((2,), jnp.int32)]
        + [shape((1, *own.shape[1:])) for _ in carry],
        compiler_params=params(1),
        name=f"encode{size}",
    )(place, counts, x, *consts, *([own] if carry else []))
    return out[: plan.tiles], *out[plan.tiles :]


def decode(plan, ns, chunk, size, nb, place, got, counts, own, other, before, consts, home, away, span, bufs, offset):
    skip, steps = chunk // nb, size // nb
    lanes = nb * plan.vregs * LANES
    flat = GRID * plan.width
    picture = pl.BlockSpec((1, 1, nb, FINE, flat), lambda s, i, at: (at[0], at[1] ^ s, skip + i, 0, 0))

    def packets(k, off):
        return pl.BlockSpec(
            (nb // 2, MID, plan.packet),
            lambda s, i, at: (off // (nb // 2) + jnp.where(s == k, i, jnp.where(s < k, 0, steps - 1)), 0, 0),
        )

    args = (*got, counts, own, other, before) + consts
    specs = (
        [packets(k, 0) for k in range(plan.tiles)]
        + [SMEM, picture, pl.BlockSpec((1, nb, FINE, flat), lambda s, i, at: (at[1] ^ s, skip + i, 0, 0)), block(before)]
        + [block(a) for a in consts]
    )
    alias = {}
    for to, array in enumerate((home, away, None, None, *(bufs or ()))):
        if array is not None:
            alias[len(args) + 1] = to
            args, specs = args + (array,), specs + [ANYWHERE]
    home, away, total, *send = pl.pallas_call(
        functools.partial(decode_kernel, plan, ns, chunk, nb, len(alias)),
        grid_spec=pltpu.PrefetchScalarGridSpec(
            num_scalar_prefetch=1,
            grid=(plan.tiles, steps),
            in_specs=specs,
            out_specs=[
                picture,
                pl.BlockSpec((1, nb, FINE, flat), lambda s, i, at: (at[1] ^ s, skip - span[0] // nb + i, 0, 0)),
                block(before),
                *[packets(k, offset if k else 0) for k in range(plan.tiles)],
            ],
            scratch_shapes=[
                pltpu.VMEM((plan.vregs, nb, FINE, 512), BF),
                pltpu.VMEM((COLS + ONES, lanes), BF),
                pltpu.VMEM((ROWS, lanes), BF),
                pltpu.VMEM((plan.vregs, nb, FINE, 512), BF),
                pltpu.VMEM((nb // 2, MID, 2 * plan.vregs * LANES), BF),
                pltpu.VMEM((nb // 2, MID, plan.packet), BF),
                pltpu.VMEM((nb // 2, MID, plan.packet), BF),
            ],
        ),
        out_shape=[
            shape(own.shape),
            shape((plan.tiles, span[1] - span[0], FINE, flat)),
            shape(before.shape, F32),
            shape((size // 2, MID, plan.packet)),
            *[shape(b.shape if bufs else (size // 2, MID, plan.packet)) for b in (bufs or got[1:])],
        ],
        input_output_aliases=alias,
        compiler_params=params(2),
        name=f"decode{size}",
    )(place, *args)
    return home, away, total, send


def back(plan, ns, chunk, size, nb, place, counts, got, offset, slope, phases, before, consts, grad):
    skip = chunk // nb
    per = 8 // plan.vregs
    args = (counts, *got, slope, phases, before) + consts
    specs = (
        [SMEM]
        + [
            pl.BlockSpec((nb // 2, MID, plan.packet), lambda i, at, off=off: (off // (nb // 2) + i, 0, 0))
            for off in [0] + [offset] * (plan.tiles - 1)
        ]
        + [
            pl.BlockSpec((nb, MID, 8 * LANES), lambda i, at: (i, 0, 0)),
            pl.BlockSpec((nb, 4 * FINE, 8 * LANES), lambda i, at: (i, 0, 0)),
            block(before),
        ]
        + [block(a) for a in consts]
    )
    alias = {}
    if grad is not None:
        alias[len(args) + 1] = 0
        args, specs = args + (grad,), specs + [ANYWHERE]
    return pl.pallas_call(
        functools.partial(back_kernel, plan, ns, chunk, nb, int(grad is not None)),
        grid_spec=pltpu.PrefetchScalarGridSpec(
            num_scalar_prefetch=1,
            grid=(size // nb,),
            in_specs=specs,
            out_specs=[
                pl.BlockSpec((nb, FINE, GRID * GRID), lambda i, at: (skip + i, 0, 0)),
                block(before),
                pl.BlockSpec((TAPS * TAPS, MID, FINE), lambda i, at: (0, 0, 0)),
            ],
            scratch_shapes=[
                pltpu.VMEM((plan.tiles, nb // 2, MID, plan.packet), BF),
                pltpu.VMEM((plan.vregs, nb, MID, plan.tiles * LANES), BF),
                pltpu.VMEM((COLS, 8 * LANES), BF),
                pltpu.VMEM((ROWS + ONES, 8 * LANES), BF),
                pltpu.VMEM((8, nb, FINE, 512), BF),
            ],
        ),
        out_shape=[
            shape((ns, FINE, GRID * GRID)),
            shape(before.shape, F32),
            shape((TAPS * TAPS, MID, FINE), F32),
        ],
        input_output_aliases=alias,
        compiler_params=params(1),
        name=f"back{size}",
    )(place, *args)


def reduce(enc, enc_total, dec, dec_bias):
    axes = tuple(lax.axis_size(name) for name in ("ga", "ty", "tx"))
    n = axes[0] * axes[1]
    size = enc.shape[1]
    piece = (32, 2 * size // n)
    sems = [pltpu.SemaphoreType.DMA((n,))] * 2 + [pltpu.SemaphoreType.DMA((axes[2],))] * 2
    return pl.pallas_call(
        functools.partial(reduce_kernel, axes),
        grid=(1,),
        in_specs=[block(enc), pl.BlockSpec((8, LANES), lambda i: (ROWS // 8, 0)), block(dec), block(dec_bias)],
        out_specs=[block(enc), block(dec), block(dec_bias), block(dec_bias)],
        out_shape=[shape(enc.shape, F32), shape(dec.shape, F32), *[shape(dec_bias.shape, F32)] * 2],
        scratch_shapes=[
            pltpu.VMEM((2, 32, size), F32),
            pltpu.VMEM((n, *piece), F32),
            pltpu.VMEM((2, 32, size), F32),
            pltpu.VMEM((axes[2], *piece), F32),
            *sems,
            *sems[:2],
        ],
        compiler_params=pltpu.CompilerParams(collective_id=0, has_side_effects=True, vmem_limit_bytes=VMEM_BYTES),
        name="reduce",
    )(enc, enc_total, dec, dec_bias)


def kernel_matrix(kernel):
    spread = jnp.pad(kernel, ((0, 0), (0, 1), (0, 0), (0, 0))).reshape(TAPS, 3, 2, FINE, MID)
    return spread.transpose(0, 2, 3, 1, 4).reshape(ROWS, COLS)


def taps_of(total):
    split = total[:, :COLS].reshape(TAPS, 2, FINE, 3, MID).transpose(0, 3, 1, 2, 4)
    return split.reshape(TAPS, 6, FINE, MID)[:, :TAPS]


def body(snapshots, counts, enc_weight, enc_bias, dec_weight, dec_bias, cotangent):
    ns = snapshots.shape[0]
    sides, tiles = lax.axis_size("ty"), lax.axis_size("tx")
    plan = Plan(tiles)
    half = tiles * ns
    ty, tx = lax.axis_index("ty"), lax.axis_index("tx")
    half_counts = lax.dynamic_slice_in_dim(counts, ty * half, half)
    sizes = [8, 16, 16, 8] if ns == 48 else [4] * (ns // 4)
    starts = [sum(sizes[:c]) for c in range(len(sizes))]
    chunks = len(sizes)
    nb = 4
    place = jnp.stack([ty, tx]).astype(jnp.int32)

    def swapped(array, axis, k):
        size = lax.axis_size(axis)
        return array if k == 0 else lax.ppermute(array, axis, [(i, i ^ k) for i in range(size)])

    split, image_join = jnp.asarray(image_split()), jnp.asarray(image_split().T)
    cot_split, cot_join = jnp.asarray(tile_split(plan)), jnp.asarray(tile_split(plan).T)
    into, out_of = jnp.asarray(to_tiles(plan)), jnp.asarray(to_tiles(plan).T)
    edges = jnp.asarray(edge_pick(plan, 0))
    spread = jnp.asarray(edge_pick(plan, 1).T)
    shifts = jnp.asarray(column_shifts(plan))
    enc = kernel_matrix(enc_weight.transpose(2, 3, 1, 0))
    dec = kernel_matrix(dec_weight.transpose(2, 3, 0, 1)[::-1, ::-1])
    enc_b = jnp.broadcast_to(enc_bias.astype(F32)[:, None], (MID, LANES))
    dec_b = jnp.broadcast_to(jnp.tile(dec_bias.astype(F32), 2)[:, None], (MID, LANES))

    enc_consts = (split, into, edges, enc.T, enc_b)
    dec_consts = (cot_split, cot_join, shifts, edges, dec, dec.T, dec_b)
    back_consts = (spread, out_of, image_join, enc)

    def pairs(c):
        return sizes[c] // 2 if 0 <= c < chunks else 0

    def run_encode(c, there, own=None):
        return encode(plan, ns, starts[c], sizes[c], nb, pairs(c - 2), there, counts, snapshots, enc_consts, own)

    own = cotangent.reshape(sides, tiles, ns, FINE, -1)
    spans = ((0, starts[-1]), (starts[-1], ns))
    home, away, arrived = None, [None, None], [None, None]
    dec_total = jnp.zeros((ROWS, 2 * LANES), F32)
    enc_total = jnp.zeros((ROWS + ONES, 2 * LANES), F32)
    grad, got, other, lent, dec_flat = None, None, None, None, None
    fronts, extras, backs = {}, {}, {}
    (fronts[0], *bufs), *extras[0], there = run_encode(0, place)
    for s in range(chunks + 3):
        sent = [swapped(bufs[k - 1], "tx", k) for k in range(tiles - 1, 0, -1)] if bufs else None
        bufs = None
        if s == 1:
            other = swapped(lent, "ty", 1)
        if 0 <= s - chunks < 2:
            arrived[s - chunks] = swapped(away[s - chunks], "ty", 1)
        if s + 1 < chunks:
            (fronts[s + 1], *bufs), *extras[s + 1], there = run_encode(s + 1, there, None if s else own)
            if s == 0:
                there, lent = extras[1].pop(), there[0]
        if 0 <= s - 1 < chunks:
            c = s - 1
            late = int(c == chunks - 1)
            home, away[late], dec_total, (backs[c], *bufs) = decode(
                plan,
                ns,
                starts[c],
                sizes[c],
                4 if sizes[c] % 8 else 8,
                place,
                [fronts[c], *got[::-1]],
                half_counts,
                own,
                other,
                dec_total,
                dec_consts,
                home,
                away[late],
                spans[late],
                bufs,
                pairs(s + 1),
            )
        if s - 3 >= 0:
            c = s - 3
            grad, enc_total, enc_taps = back(
                plan,
                ns,
                starts[c],
                sizes[c],
                nb,
                place,
                counts,
                [backs[c], *got[::-1]],
                pairs(s - 1),
                *extras[c],
                enc_total,
                back_consts,
                grad,
            )
        if s == chunks:
            dec_taps = taps_of(dec_total)[::-1, ::-1].reshape(25, FINE * MID)
            dec_bias_part = dec_total[2 * MID : 4 * MID, COLS].reshape(4, FINE).sum(0)
            dec_bias_part = jnp.pad(dec_bias_part[None], ((0, 0), (0, LANES - FINE)))
            dec_flat = (dec_taps, dec_bias_part)
        for late in range(2):
            if s == chunks + 1 + late:
                home = lax.dynamic_update_slice(home, arrived[late][None], (1 - ty, 0, spans[late][0], 0, 0))
        if s < chunks + 2:
            state = (sent, bufs, fronts, home, away, arrived, dec_total, grad, enc_total, dec_flat, there, lent)
            state = lax.optimization_barrier(state)
            got, bufs, fronts, home, away, arrived, dec_total, grad, enc_total, dec_flat, there, lent = state
    enc_weight_grad, dec_weight_grad, enc_bias_grad, dec_bias_grad = reduce(
        enc_taps.reshape(25, MID * FINE), enc_total, *dec_flat
    )
    enc_bias_grad, dec_bias_grad = enc_bias_grad[0, MID:], dec_bias_grad[0, :FINE]
    decoded = home.reshape(cotangent.shape)
    return (decoded, grad, enc_weight_grad, enc_bias_grad, dec_weight_grad, dec_bias_grad)


def solution(mesh):
    return jax.shard_map(
        body,
        mesh=mesh,
        in_specs=(
            P(("ga", "ty", "tx"), None, None),
            P("ga"),
            P(),
            P(),
            P(),
            P(),
            P("ga", None, "ty", "tx", None),
        ),
        out_specs=(
            P("ga", None, "ty", "tx", None),
            P(("ga", "ty", "tx"), None, None),
            P(),
            P(),
            P(),
            P(),
        ),
        check_vma=False,
    )
```

```python
import functools

import jax
import jax.numpy as jnp
import ml_dtypes
import numpy as np
from jax import lax
from jax.experimental import pallas as pl
from jax.experimental.pallas import tpu as pltpu
from jax.sharding import PartitionSpec as P


FINE = 32
MID = 64
GRID = 64
COARSE = 32
LANES = 128
TAPS = 5
ROWS = TAPS * 2 * FINE
COLS = 3 * MID
ONES = 16
UNIT = 4
BF = jnp.bfloat16
F32 = jnp.float32
VMEM_BYTES = 56 * 1024 * 1024


class Plan:
    def __init__(self, tiles):
        self.tiles = tiles
        self.width = COARSE // tiles
        self.vregs = COARSE * self.width // LANES
        self.rows = LANES // self.width
        self.packet = 2 * self.vregs * LANES + LANES


def one(matrix):
    return matrix.astype(ml_dtypes.bfloat16)


def image_split():
    out = np.zeros((4, 2, 32, 2, 2, 2, 4, 32), np.float32)
    for m in range(4):
        for pr in range(2):
            for j in range(32):
                for pc in range(2):
                    out[m, pr, j, pc, pr, pc, m, j] = 1
    return one(out.reshape(512, 512))


def tile_split(plan):
    n, w = plan.rows, plan.width
    out = np.zeros((n, 2, w, 2, 2, 2, n, w), np.float32)
    for i in range(n):
        for pr in range(2):
            for j in range(w):
                for pc in range(2):
                    out[i, pr, j, pc, pr, pc, i, j] = 1
    return one(out.reshape(512, 512))


def to_tiles(plan):
    halves = 2 // plan.vregs
    out = np.zeros((halves, 4, 4, plan.tiles, plan.width, plan.tiles, halves, 4, 4, plan.width), np.float32)
    for r in range(halves):
        for u in range(4):
            for m in range(4):
                for t in range(plan.tiles):
                    for j in range(plan.width):
                        out[r, u, m, t, j, t, r, m, u, j] = 1
    size = halves * 4 * LANES
    return one(out.reshape(size, size))


def edge_pick(plan, swap):
    v, n, w = plan.vregs, plan.rows, plan.width
    out = np.zeros((2, v, n, w, 2, v, 2, n), np.float32)
    for p in range(2):
        for q in range(v):
            for i in range(n):
                for edge in range(2):
                    out[p, q, i, (w - 1) * (edge ^ swap), p, q, edge, i] = 1
    return one(out.reshape(2 * v * LANES, LANES))


def column_shifts(plan):
    v, n, w = plan.vregs, plan.rows, plan.width
    out = np.zeros((2, v, 2, LANES, 2, n, w), np.float32)
    for p in range(2):
        for q in range(v):
            for i in range(n):
                for j in range(w):
                    if j < w - 1:
                        out[p, q, 0, i * w + j + 1, 0, i, j] = 1
                    else:
                        out[p, q, 1, ((p * v + q) * 2 + 0) * n + i, 0, i, j] = 1
                    if j > 0:
                        out[p, q, 0, i * w + j - 1, 1, i, j] = 1
                    else:
                        out[p, q, 1, ((p * v + q) * 2 + 1) * n + i, 1, i, j] = 1
    return one(out.reshape(2 * v, 2 * LANES, 2 * LANES))


def dot(a, b):
    return jnp.dot(a, b, preferred_element_type=F32)


def dot_nt(a, b):
    return lax.dot_general(a, b, (((1,), (1,)), ((), ())), preferred_element_type=F32)


def lane_of(rows):
    return lax.broadcasted_iota(jnp.int32, (rows, LANES), 1)


def turn(x, by):
    return pltpu.roll(x, (-by) % LANES, 1)


def shift_rows(pieces, d, halves, inner, step):
    lane = lane_of(pieces[0].shape[0])
    out = []
    for r in range(halves):
        for u in range(inner):
            if 0 <= u + d < inner:
                out.append(pieces[r * inner + u + d])
            elif d > 0:
                here = turn(pieces[r * inner], step)
                after = turn(pieces[(r + 1) * inner], step) if r + 1 < halves else 0.0
                out.append(jnp.where(lane < LANES - step, here, after))
            else:
                here = turn(pieces[r * inner + inner - 1], -step)
                before = turn(pieces[r * inner - 1], -step) if r else 0.0
                out.append(jnp.where(lane >= step, here, before))
    return out


def shift_cols(x, d, width):
    j = lane_of(x.shape[0]) & (width - 1)
    return jnp.where(j < width - 1 if d > 0 else j >= 1, turn(x, d), 0.0)


def tap_of(t):
    return t % 2, t // 2 - 1


def up_rows(q, parity, halves, inner, step):
    total = None
    for t in range(parity, TAPS, 2):
        d = -tap_of(t)[1]
        part = q[t] if d == 0 else shift_rows(q[t], d, halves, inner, step)
        total = part if total is None else [a + b for a, b in zip(total, part)]
    return total


def kept(count):
    return lax.broadcasted_iota(jnp.int32, (FINE, LANES), 0) // (FINE // 4) < count


def encode_kernel(plan, ns, chunk, nb, carried, place, counts, x, split, tiles, edges, weights_t, bias, *rest):
    refs, rest = rest[:carried], rest[carried:]
    send, (slope, phases, there, *rest) = rest[: plan.tiles], rest[plan.tiles :]
    refs, (lx, rows, lt, lc, stage) = (*refs, *rest[:carried]), rest[carried:]
    there[0], there[1] = place[0], place[1]
    first = (place[0] * plan.tiles + place[1]) * ns + chunk + pl.program_id(0) * nb
    tx = place[1]
    width, vregs, per = plan.width, plan.vregs, 8 // plan.vregs
    if carried:
        refs[-1][...] = refs[-2][...]
    for n in range(nb):
        keep = kept(counts[first + n]).astype(BF)
        for i in range(COARSE):
            r, m, u = i // 16, i % 16 // 4, i % 4
            lx[r * 4 + u, n, :, m * LANES : (m + 1) * LANES] = x[n, :, i * LANES : (i + 1) * LANES] * keep
    y = dot(lx[...].reshape(8 * nb * FINE, 512), split[...])
    for n in range(nb):
        for ph in range(4):
            pr, pc = ph // 2, ph % 2
            pieces = [
                y[(v * nb + n) * FINE : (v * nb + n + 1) * FINE, ph * LANES : (ph + 1) * LANES] for v in range(8)
            ]
            for v in range(8):
                phases[n, ph * FINE : (ph + 1) * FINE, v * LANES : (v + 1) * LANES] = pieces[v].astype(BF)
            for t in range(pr, TAPS, 2):
                d = tap_of(t)[1]
                moved = shift_rows(pieces, d, 2, 4, COARSE)
                at = (t * 2 + pc) * FINE
                for v in range(8):
                    rows[at : at + FINE, v * LANES : (v + 1) * LANES] = moved[v].astype(BF)
        s = dot(weights_t[...], rows[...])
        for v in range(8):
            cut = slice(v * LANES, (v + 1) * LANES)
            pre = s[MID : 2 * MID, cut] + bias[...]
            pre += shift_cols(s[:MID, cut], -1, COARSE) + shift_cols(s[2 * MID :, cut], 1, COARSE)
            e = jnp.exp(jnp.minimum(pre, 0.0))
            slope[n, :, cut] = e.astype(BF)
            hidden = jnp.where(pre > 0, pre, e - 1.0).astype(BF)
            w, at = v // per, v % per
            lt[w, n, :, at * LANES : (at + 1) * LANES] = hidden
    z = dot(lt[...].reshape(vregs * nb * MID, per * LANES), tiles[...])
    j = lane_of(MID) & (width - 1)
    for n in range(nb):
        for w in range(vregs):
            at = (w * nb + n) * MID
            main = [z[at : at + MID, t * LANES : (t + 1) * LANES] for t in range(plan.tiles)]
            cut = slice((n % 2 * vregs + w) * LANES, (n % 2 * vregs + w + 1) * LANES)
            for t in range(plan.tiles):
                stage[t, n // 2, :, cut] = main[t].astype(BF)
                left = main[t - 1] if t else 0.0
                right = main[t + 1] if t + 1 < plan.tiles else 0.0
                rim = jnp.where(j == 0, right, jnp.where(j == width - 1, left, 0.0))
                lc[t, n // 2, :, cut] = rim.astype(BF)
    rims = dot(lc[...].reshape(plan.tiles * nb // 2 * MID, 2 * vregs * LANES), edges[...])
    for t in range(plan.tiles):
        for pair in range(nb // 2):
            at = (t * nb // 2 + pair) * MID
            stage[t, pair, :, 2 * vregs * LANES :] = rims[at : at + MID].astype(BF)
    for k in range(plan.tiles):
        send[k][...] = stage[tx ^ k]


def decode_kernel(plan, ns, chunk, nb, chained, place, *refs):
    parts, refs = refs[: plan.tiles], refs[plan.tiles :]
    counts, own, other, before, split, join, shifts, edges, weights, weights_t, bias = refs[:11]
    home, away, total, *refs = refs[11 + chained :]
    sends, (lcot, cols, rows, ldec, lc, got, send) = refs[: plan.tiles], refs[plan.tiles :]
    ty, part, step = place[0], pl.program_id(0), pl.program_id(1)
    upper = ty == 0
    first = (place[1] ^ part) * ns + chunk + step * nb
    width, vregs = plan.width, plan.vregs
    edge_at = 2 * vregs * LANES
    masks = [kept(counts[first + n]) for n in range(nb)]

    @pl.when((part == 0) & (step == 0))
    def _():
        total[...] = before[...]

    for k in range(plan.tiles):

        @pl.when(part == k)
        def _():
            got[...] = parts[k][...]

    half = 2 // vregs
    span = 4 // half
    for n in range(nb):
        keep = masks[n].astype(BF)
        for k in range(span):
            cut = slice(k * LANES, (k + 1) * LANES)
            mine, theirs = own[0, 0, n, :, cut] * keep, other[0, n, :, cut] * keep
            for side in range(2):
                k_to = k + side % half * span
                lcot[side // half, n, :, k_to * LANES : (k_to + 1) * LANES] = (
                    jnp.where(upper, mine, theirs) if side == 0 else jnp.where(upper, theirs, mine)
                )
    c = dot(lcot[...].reshape(vregs * nb * FINE, 512), split[...])
    for p in range(2):
        for w in range(vregs):
            slot = p * vregs + w
            at = slice(slot * LANES, (slot + 1) * LANES)
            both = jnp.concatenate([got[:, :, at], got[:, :, edge_at:]], axis=2)
            moved = dot(both.reshape(nb // 2 * MID, 2 * LANES), shifts[slot]).astype(BF)
            for pair in range(nb // 2):
                lanes = slice(((2 * pair + p) * vregs + w) * LANES, ((2 * pair + p) * vregs + w + 1) * LANES)
                sub = slice(pair * MID, (pair + 1) * MID)
                cols[:MID, lanes] = moved[sub, :LANES]
                cols[MID : 2 * MID, lanes] = got[pair, :, at]
                cols[2 * MID : COLS, lanes] = moved[sub, LANES:]
    cols[COLS:, :] = jnp.ones((ONES, nb * vregs * LANES), BF)
    q = dot(weights[...], cols[:COLS, :])
    for n in range(nb):
        for pr in range(2):
            reg = {
                t: [
                    q[t * MID : (t + 1) * MID, (n * vregs + w) * LANES : (n * vregs + w + 1) * LANES]
                    for w in range(vregs)
                ]
                for t in range(pr, TAPS, 2)
            }
            pre = [x + bias[...] for x in up_rows(reg, pr, vregs, 1, width)]
            grads = []
            for w in range(vregs):
                e = jnp.exp(jnp.minimum(pre[w], 0.0))
                at = (w * nb + n) * FINE
                tangent = jnp.concatenate(
                    [
                        c[at : at + FINE, (2 * pr + pc) * LANES : (2 * pr + pc + 1) * LANES]
                        for pc in range(2)
                    ],
                    axis=0,
                )
                grads.append(tangent * e)
                out = jnp.where(pre[w] > 0, pre[w], e - 1.0).astype(BF)
                for pc in range(2):
                    cut = slice((2 * pr + pc) * LANES, (2 * pr + pc + 1) * LANES)
                    ldec[w, n, :, cut] = out[pc * FINE : (pc + 1) * FINE]
            for t in range(pr, TAPS, 2):
                moved = grads if t // 2 == 1 else shift_rows(grads, tap_of(t)[1], vregs, 1, width)
                for w in range(vregs):
                    lanes = slice((n * vregs + w) * LANES, (n * vregs + w + 1) * LANES)
                    rows[t * MID : (t + 1) * MID, lanes] = moved[w].astype(BF)
    nat = dot(ldec[...].reshape(vregs * nb * FINE, 512), join[...])
    for n in range(nb):
        for k in range(span):
            sides = []
            for side in range(2):
                at = (side // half * nb + n) * FINE
                k_from = k + side % half * span
                sides.append(jnp.where(masks[n], nat[at : at + FINE, k_from * LANES : (k_from + 1) * LANES], 0.0))
            cut = slice(k * LANES, (k + 1) * LANES)
            home[0, 0, n, :, cut] = jnp.where(upper, sides[0], sides[1]).astype(BF)
            away[0, n, :, cut] = jnp.where(upper, sides[1], sides[0]).astype(BF)
    s = dot(weights_t[...], rows[...])
    j = lane_of(MID) & (width - 1)
    for n in range(nb):
        for w in range(vregs):
            lanes = slice((n * vregs + w) * LANES, (n * vregs + w + 1) * LANES)
            behind, here, ahead = s[:MID, lanes], s[MID : 2 * MID, lanes], s[2 * MID :, lanes]
            grad = here + shift_cols(behind, -1, width) + shift_cols(ahead, 1, width)
            slot = n % 2 * vregs + w
            cut = slice(slot * LANES, (slot + 1) * LANES)
            send[n // 2, :, cut] = grad.astype(BF)
            lc[n // 2, :, cut] = jnp.where(j == 0, ahead, behind).astype(BF)
    rims = dot(lc[...].reshape(nb // 2 * MID, edge_at), edges[...])
    for pair in range(nb // 2):
        send[pair, :, edge_at:] = rims[pair * MID : (pair + 1) * MID].astype(BF)
    total[:, : COLS + ONES] += dot_nt(rows[...], cols[...])
    for k in range(plan.tiles):

        @pl.when(part == k)
        def _():
            sends[k][...] = send[...]


def back_kernel(plan, ns, chunk, nb, chained, place, counts, *refs):
    parts, refs = refs[: plan.tiles], refs[plan.tiles :]
    slope, phases, before, spread, untile, join, weights = refs[:7]
    grad, total, taps, got, lu, cols, rows, lo = refs[7 + chained :]
    step = pl.program_id(0)
    first = (place[0] * plan.tiles + place[1]) * ns + chunk + step * nb
    tx = place[1]
    width, vregs, per = plan.width, plan.vregs, 8 // plan.vregs
    edge_at = 2 * vregs * LANES

    @pl.when(step == 0)
    def _():
        total[...] = before[...]

    for k in range(plan.tiles):
        got[tx ^ k] = parts[k][...]
    rims = dot(got[:, :, :, edge_at:].reshape(plan.tiles * nb // 2 * MID, LANES), spread[...])
    j = lane_of(MID) & (width - 1)
    for n in range(nb):
        for w in range(vregs):
            slot = n % 2 * vregs + w
            cut = slice(slot * LANES, (slot + 1) * LANES)
            rim = [
                rims[(t * nb // 2 + n // 2) * MID : (t * nb // 2 + n // 2 + 1) * MID, cut] for t in range(plan.tiles)
            ]
            for t in range(plan.tiles):
                main = got[t, n // 2, :, cut].astype(F32)
                if t + 1 < plan.tiles:
                    main += jnp.where(j == width - 1, rim[t + 1], 0.0)
                if t:
                    main += jnp.where(j == 0, rim[t - 1], 0.0)
                lu[w, n, :, t * LANES : (t + 1) * LANES] = main.astype(BF)
    g = dot(lu[...].reshape(vregs * nb * MID, plan.tiles * LANES), untile[...])
    rows[ROWS:, :] = jnp.ones((ONES, 8 * LANES), BF)
    for n in range(nb):
        for v in range(8):
            lanes = slice(v * LANES, (v + 1) * LANES)
            w, at = v // per, v % per
            base = (w * nb + n) * MID
            here = g[base : base + MID, at * LANES : (at + 1) * LANES] * slope[n, :, lanes].astype(F32)
            here = here.astype(BF).astype(F32)
            cols[:MID, lanes] = shift_cols(here, 1, COARSE).astype(BF)
            cols[MID : 2 * MID, lanes] = here.astype(BF)
            cols[2 * MID : COLS, lanes] = shift_cols(here, -1, COARSE).astype(BF)
        q = dot(weights[...], cols[...])
        for pr in range(2):
            reg = {
                t: [q[t * MID : (t + 1) * MID, v * LANES : (v + 1) * LANES] for v in range(8)]
                for t in range(pr, TAPS, 2)
            }
            fine = up_rows(reg, pr, 2, 4, COARSE)
            for v in range(8):
                out = fine[v].astype(BF)
                for pc in range(2):
                    cut = slice((2 * pr + pc) * LANES, (2 * pr + pc + 1) * LANES)
                    lo[v, n, :, cut] = out[pc * FINE : (pc + 1) * FINE]
            source = [
                phases[n, pr * 2 * FINE : (pr + 1) * 2 * FINE, v * LANES : (v + 1) * LANES].astype(F32)
                for v in range(8)
            ]
            for t in range(pr, TAPS, 2):
                moved = source if t // 2 == 1 else shift_rows(source, tap_of(t)[1], 2, 4, COARSE)
                for v in range(8):
                    rows[t * MID : (t + 1) * MID, v * LANES : (v + 1) * LANES] = moved[v].astype(BF)
        total[:, :COLS] += dot_nt(rows[...], cols[...])
    nat = dot(lo[...].reshape(8 * nb * FINE, 512), join[...])
    for n in range(nb):
        keep = kept(counts[first + n])
        for i in range(COARSE):
            r, m, u = i // 16, i % 16 // 4, i % 4
            at = ((r * 4 + u) * nb + n) * FINE
            piece = jnp.where(keep, nat[at : at + FINE, m * LANES : (m + 1) * LANES], 0.0)
            grad[n, :, i * LANES : (i + 1) * LANES] = piece.astype(BF)

    @pl.when(step == pl.num_programs(0) - 1)
    def _():
        for t in range(TAPS):
            for s in range(TAPS):
                at = (2 * t + s % 2) * FINE
                tap = total[at : at + FINE, s // 4 * LANES : (s // 4 + 1) * LANES]
                if s // 2 == 1:
                    tap = turn(tap, MID)
                taps[TAPS * t + s] = tap.T[:MID]


def reduce_kernel(axes, enc, enc_bias, dec, dec_bias, *refs):
    outs, (packed, parts, full, far), sems = refs[:4], refs[4:8], refs[8:]
    n_ga, n_ty, n_tx = axes
    ga, ty, tx = lax.axis_index("ga"), lax.axis_index("ty"), lax.axis_index("tx")
    me, n = ga * n_ty + ty, n_ga * n_ty
    lanes = 2 * enc.shape[1] // n

    def near(d):
        to = (me + d) % n
        return to, {"ga": to // n_ty, "ty": to % n_ty}

    def along(d):
        return {"tx": (tx + d) % n_tx}

    def piece(ref, p, h):
        at = pl.multiple_of(p % (n // 2) * lanes, LANES)
        return ref.at[p // (n // 2), pl.ds(16 * h, 16), pl.ds(at, lanes)]

    def part(ref, d, h):
        return ref.at[d, pl.ds(16 * h, 16)]

    barrier = pltpu.get_barrier_semaphore()
    for d in range(1, n):
        pl.semaphore_signal(barrier, inc=1, device_id=near(d)[1], device_id_type=pl.DeviceIdType.MESH)
    for d in range(1, n_tx):
        pl.semaphore_signal(barrier, inc=1, device_id=along(d), device_id_type=pl.DeviceIdType.MESH)
    packed[:, 24:] = jnp.zeros((2, 8, enc.shape[1]), F32)
    packed[0, :25] = enc[...]
    packed[1, :25] = dec[...]
    packed[0, 25:26, :LANES] = enc_bias[:1]
    packed[1, 25:26, :LANES] = dec_bias[...]
    pl.semaphore_wait(barrier, n - 1 + n_tx - 1)

    def begin(h, peers, source, target, send, recv):
        copies = [
            pltpu.make_async_remote_copy(
                src_ref=source(d),
                dst_ref=target(d),
                send_sem=send.at[h, d],
                recv_sem=recv.at[h, d],
                device_id=to,
                device_id_type=pl.DeviceIdType.MESH,
            )
            for d, to in peers
        ]
        for copy in copies:
            copy.start()
        return copies

    def end(copies):
        for copy in copies:
            copy.wait()

    plane, line = [(d, near(d)[1]) for d in range(1, n)], [(d, along(d)) for d in range(1, n_tx)]
    halves = (0, 1)
    flying = [
        begin(h, plane, lambda d: piece(packed, near(d)[0], h), lambda d: part(parts, d, h), sems[0], sems[1])
        for h in halves
    ]
    for h in halves:
        end(flying[h])
        mine = piece(packed, me, h)[...]
        for d in range(1, n):
            mine = mine + part(parts, d, h)[...]
        part(far, tx, h)[...] = mine
        flying[h] = begin(
            h, line, lambda d: part(far, tx, h), lambda d: part(far, tx, h), sems[2], sems[3]
        )
    for h in halves:
        end(flying[h])
        mine = part(far, 0, h)[...]
        for t in range(1, n_tx):
            mine = mine + part(far, t, h)[...]
        piece(full, me, h)[...] = mine
        flying[h] = begin(
            h, plane, lambda d: piece(full, me, h), lambda d: piece(full, me, h), sems[4], sems[5]
        )
    for h in halves:
        end(flying[h])
    outs[0][...] = full[0, :25]
    outs[1][...] = full[1, :25]
    outs[2][...] = full[0, 25:26, :LANES]
    outs[3][...] = full[1, 25:26, :LANES]


def block(array):
    return pl.BlockSpec(array.shape, lambda *_: (0,) * array.ndim)


SMEM = pl.BlockSpec(memory_space=pltpu.SMEM)
ANYWHERE = pl.BlockSpec(memory_space=pl.ANY)


def params(steps):
    return pltpu.CompilerParams(dimension_semantics=("arbitrary",) * steps, vmem_limit_bytes=VMEM_BYTES)


def shape(dims, dtype=BF):
    return jax.ShapeDtypeStruct(dims, dtype)


def encode(plan, ns, chunk, size, nb, extra, place, counts, x, consts, own=None):
    per, skip, steps = 8 // plan.vregs, chunk // nb, size // nb
    packets = pl.BlockSpec((nb // 2, MID, plan.packet), lambda i, at: (i, 0, 0))
    carry, carried = [], []
    if own is not None:
        dims = (plan.tiles // steps, *own.shape[2:])
        carry = [pl.BlockSpec((1, *dims), lambda i, at: (1 - at[0], i, 0, 0, 0))]
        carried = [pl.BlockSpec((1, *dims), lambda i, at: (0, i, 0, 0, 0))]
    out = pl.pallas_call(
        functools.partial(encode_kernel, plan, ns, chunk, nb, len(carry)),
        grid_spec=pltpu.PrefetchScalarGridSpec(
            num_scalar_prefetch=1,
            grid=(steps,),
            in_specs=[SMEM, pl.BlockSpec((nb, FINE, GRID * GRID), lambda i, at: (skip + i, 0, 0))]
            + [block(a) for a in consts]
            + carry,
            out_specs=[packets] * plan.tiles
            + [
                pl.BlockSpec((nb, MID, 8 * LANES), lambda i, at: (i, 0, 0)),
                pl.BlockSpec((nb, 4 * FINE, 8 * LANES), lambda i, at: (i, 0, 0)),
                SMEM,
            ]
            + carried,
            scratch_shapes=[
                pltpu.VMEM((8, nb, FINE, 512), BF),
                pltpu.VMEM((ROWS, 8 * LANES), BF),
                pltpu.VMEM((plan.vregs, nb, MID, per * LANES), BF),
                pltpu.VMEM((plan.tiles, nb // 2, MID, 2 * plan.vregs * LANES), BF),
                pltpu.VMEM((plan.tiles, nb // 2, MID, plan.packet), BF),
            ],
        ),
        out_shape=[shape((size // 2 + (extra if k else 0), MID, plan.packet)) for k in range(plan.tiles)]
        + [shape((size, MID, 8 * LANES)), shape((size, 4 * FINE, 8 * LANES)), shape((2,), jnp.int32)]
        + [shape((1, *own.shape[1:])) for _ in carry],
        compiler_params=params(1),
        name=f"encode{size}",
    )(place, counts, x, *consts, *([own] if carry else []))
    return out[: plan.tiles], *out[plan.tiles :]


def decode(plan, ns, chunk, size, nb, place, got, counts, own, other, before, consts, home, away, span, bufs, offset):
    skip, steps = chunk // nb, size // nb
    lanes = nb * plan.vregs * LANES
    flat = GRID * plan.width
    picture = pl.BlockSpec((1, 1, nb, FINE, flat), lambda s, i, at: (at[0], at[1] ^ s, skip + i, 0, 0))

    def packets(k, off):
        return pl.BlockSpec(
            (nb // 2, MID, plan.packet),
            lambda s, i, at: (off // (nb // 2) + jnp.where(s == k, i, jnp.where(s < k, 0, steps - 1)), 0, 0),
        )

    args = (*got, counts, own, other, before) + consts
    specs = (
        [packets(k, 0) for k in range(plan.tiles)]
        + [SMEM, picture, pl.BlockSpec((1, nb, FINE, flat), lambda s, i, at: (at[1] ^ s, skip + i, 0, 0)), block(before)]
        + [block(a) for a in consts]
    )
    alias = {}
    for to, array in enumerate((home, away, None, None, *(bufs or ()))):
        if array is not None:
            alias[len(args) + 1] = to
            args, specs = args + (array,), specs + [ANYWHERE]
    home, away, total, *send = pl.pallas_call(
        functools.partial(decode_kernel, plan, ns, chunk, nb, len(alias)),
        grid_spec=pltpu.PrefetchScalarGridSpec(
            num_scalar_prefetch=1,
            grid=(plan.tiles, steps),
            in_specs=specs,
            out_specs=[
                picture,
                pl.BlockSpec((1, nb, FINE, flat), lambda s, i, at: (at[1] ^ s, skip - span[0] // nb + i, 0, 0)),
                block(before),
                *[packets(k, offset if k else 0) for k in range(plan.tiles)],
            ],
            scratch_shapes=[
                pltpu.VMEM((plan.vregs, nb, FINE, 512), BF),
                pltpu.VMEM((COLS + ONES, lanes), BF),
                pltpu.VMEM((ROWS, lanes), BF),
                pltpu.VMEM((plan.vregs, nb, FINE, 512), BF),
                pltpu.VMEM((nb // 2, MID, 2 * plan.vregs * LANES), BF),
                pltpu.VMEM((nb // 2, MID, plan.packet), BF),
                pltpu.VMEM((nb // 2, MID, plan.packet), BF),
            ],
        ),
        out_shape=[
            shape(own.shape),
            shape((plan.tiles, span[1] - span[0], FINE, flat)),
            shape(before.shape, F32),
            shape((size // 2, MID, plan.packet)),
            *[shape(b.shape if bufs else (size // 2, MID, plan.packet)) for b in (bufs or got[1:])],
        ],
        input_output_aliases=alias,
        compiler_params=params(2),
        name=f"decode{size}",
    )(place, *args)
    return home, away, total, send


def back(plan, ns, chunk, size, nb, place, counts, got, offset, slope, phases, before, consts, grad):
    skip = chunk // nb
    per = 8 // plan.vregs
    args = (counts, *got, slope, phases, before) + consts
    specs = (
        [SMEM]
        + [
            pl.BlockSpec((nb // 2, MID, plan.packet), lambda i, at, off=off: (off // (nb // 2) + i, 0, 0))
            for off in [0] + [offset] * (plan.tiles - 1)
        ]
        + [
            pl.BlockSpec((nb, MID, 8 * LANES), lambda i, at: (i, 0, 0)),
            pl.BlockSpec((nb, 4 * FINE, 8 * LANES), lambda i, at: (i, 0, 0)),
            block(before),
        ]
        + [block(a) for a in consts]
    )
    alias = {}
    if grad is not None:
        alias[len(args) + 1] = 0
        args, specs = args + (grad,), specs + [ANYWHERE]
    return pl.pallas_call(
        functools.partial(back_kernel, plan, ns, chunk, nb, int(grad is not None)),
        grid_spec=pltpu.PrefetchScalarGridSpec(
            num_scalar_prefetch=1,
            grid=(size // nb,),
            in_specs=specs,
            out_specs=[
                pl.BlockSpec((nb, FINE, GRID * GRID), lambda i, at: (skip + i, 0, 0)),
                block(before),
                pl.BlockSpec((TAPS * TAPS, MID, FINE), lambda i, at: (0, 0, 0)),
            ],
            scratch_shapes=[
                pltpu.VMEM((plan.tiles, nb // 2, MID, plan.packet), BF),
                pltpu.VMEM((plan.vregs, nb, MID, plan.tiles * LANES), BF),
                pltpu.VMEM((COLS, 8 * LANES), BF),
                pltpu.VMEM((ROWS + ONES, 8 * LANES), BF),
                pltpu.VMEM((8, nb, FINE, 512), BF),
            ],
        ),
        out_shape=[
            shape((ns, FINE, GRID * GRID)),
            shape(before.shape, F32),
            shape((TAPS * TAPS, MID, FINE), F32),
        ],
        input_output_aliases=alias,
        compiler_params=params(1),
        name=f"back{size}",
    )(place, *args)


def reduce(enc, enc_total, dec, dec_bias):
    axes = tuple(lax.axis_size(name) for name in ("ga", "ty", "tx"))
    n = axes[0] * axes[1]
    size = enc.shape[1]
    piece = (32, 2 * size // n)
    sems = [pltpu.SemaphoreType.DMA((2, n))] * 2 + [pltpu.SemaphoreType.DMA((2, axes[2]))] * 2
    return pl.pallas_call(
        functools.partial(reduce_kernel, axes),
        grid=(1,),
        in_specs=[block(enc), pl.BlockSpec((8, LANES), lambda i: (ROWS // 8, 0)), block(dec), block(dec_bias)],
        out_specs=[block(enc), block(dec), block(dec_bias), block(dec_bias)],
        out_shape=[shape(enc.shape, F32), shape(dec.shape, F32), *[shape(dec_bias.shape, F32)] * 2],
        scratch_shapes=[
            pltpu.VMEM((2, 32, size), F32),
            pltpu.VMEM((n, *piece), F32),
            pltpu.VMEM((2, 32, size), F32),
            pltpu.VMEM((axes[2], *piece), F32),
            *sems,
            *sems[:2],
        ],
        compiler_params=pltpu.CompilerParams(collective_id=0, has_side_effects=True, vmem_limit_bytes=VMEM_BYTES),
        name="reduce",
    )(enc, enc_total, dec, dec_bias)


def kernel_matrix(kernel):
    spread = jnp.pad(kernel, ((0, 0), (0, 1), (0, 0), (0, 0))).reshape(TAPS, 3, 2, FINE, MID)
    return spread.transpose(0, 2, 3, 1, 4).reshape(ROWS, COLS)


def taps_of(total):
    split = total[:, :COLS].reshape(TAPS, 2, FINE, 3, MID).transpose(0, 3, 1, 2, 4)
    return split.reshape(TAPS, 6, FINE, MID)[:, :TAPS]


def body(snapshots, counts, enc_weight, enc_bias, dec_weight, dec_bias, cotangent):
    ns = snapshots.shape[0]
    sides, tiles = lax.axis_size("ty"), lax.axis_size("tx")
    plan = Plan(tiles)
    half = tiles * ns
    ty, tx = lax.axis_index("ty"), lax.axis_index("tx")
    half_counts = lax.dynamic_slice_in_dim(counts, ty * half, half)
    sizes = [8, 16, 16, 8] if ns == 48 else [4] * (ns // 4)
    starts = [sum(sizes[:c]) for c in range(len(sizes))]
    chunks = len(sizes)
    nb = 4
    place = jnp.stack([ty, tx]).astype(jnp.int32)

    def swapped(array, axis, k):
        size = lax.axis_size(axis)
        return array if k == 0 else lax.ppermute(array, axis, [(i, i ^ k) for i in range(size)])

    split, image_join = jnp.asarray(image_split()), jnp.asarray(image_split().T)
    cot_split, cot_join = jnp.asarray(tile_split(plan)), jnp.asarray(tile_split(plan).T)
    into, out_of = jnp.asarray(to_tiles(plan)), jnp.asarray(to_tiles(plan).T)
    edges = jnp.asarray(edge_pick(plan, 0))
    spread = jnp.asarray(edge_pick(plan, 1).T)
    shifts = jnp.asarray(column_shifts(plan))
    enc = kernel_matrix(enc_weight.transpose(2, 3, 1, 0))
    dec = kernel_matrix(dec_weight.transpose(2, 3, 0, 1)[::-1, ::-1])
    enc_b = jnp.broadcast_to(enc_bias.astype(F32)[:, None], (MID, LANES))
    dec_b = jnp.broadcast_to(jnp.tile(dec_bias.astype(F32), 2)[:, None], (MID, LANES))

    enc_consts = (split, into, edges, enc.T, enc_b)
    dec_consts = (cot_split, cot_join, shifts, edges, dec, dec.T, dec_b)
    back_consts = (spread, out_of, image_join, enc)

    def pairs(c):
        return sizes[c] // 2 if 0 <= c < chunks else 0

    def run_encode(c, there, own=None):
        return encode(plan, ns, starts[c], sizes[c], nb, pairs(c - 2), there, counts, snapshots, enc_consts, own)

    own = cotangent.reshape(sides, tiles, ns, FINE, -1)
    spans = ((0, starts[-1]), (starts[-1], ns))
    home, away, arrived = None, [None, None], [None, None]
    dec_total = jnp.zeros((ROWS, 2 * LANES), F32)
    enc_total = jnp.zeros((ROWS + ONES, 2 * LANES), F32)
    grad, got, other, lent, dec_flat = None, None, None, None, None
    fronts, extras, backs = {}, {}, {}
    (fronts[0], *bufs), *extras[0], there = run_encode(0, place)
    for s in range(chunks + 3):
        sent = [swapped(bufs[k - 1], "tx", k) for k in range(tiles - 1, 0, -1)] if bufs else None
        bufs = None
        if s == 1:
            other = swapped(lent, "ty", 1)
        if 0 <= s - chunks < 2:
            arrived[s - chunks] = swapped(away[s - chunks], "ty", 1)
        if s + 1 < chunks:
            (fronts[s + 1], *bufs), *extras[s + 1], there = run_encode(s + 1, there, None if s else own)
            if s == 0:
                there, lent = extras[1].pop(), there[0]
        if 0 <= s - 1 < chunks:
            c = s - 1
            late = int(c == chunks - 1)
            home, away[late], dec_total, (backs[c], *bufs) = decode(
                plan,
                ns,
                starts[c],
                sizes[c],
                4 if sizes[c] % 8 else 8,
                place,
                [fronts[c], *got[::-1]],
                half_counts,
                own,
                other,
                dec_total,
                dec_consts,
                home,
                away[late],
                spans[late],
                bufs,
                pairs(s + 1),
            )
        if s - 3 >= 0:
            c = s - 3
            grad, enc_total, enc_taps = back(
                plan,
                ns,
                starts[c],
                sizes[c],
                nb,
                place,
                counts,
                [backs[c], *got[::-1]],
                pairs(s - 1),
                *extras[c],
                enc_total,
                back_consts,
                grad,
            )
        if s == chunks:
            dec_taps = taps_of(dec_total)[::-1, ::-1].reshape(25, FINE * MID)
            dec_bias_part = dec_total[2 * MID : 4 * MID, COLS].reshape(4, FINE).sum(0)
            dec_bias_part = jnp.pad(dec_bias_part[None], ((0, 0), (0, LANES - FINE)))
            dec_flat = (dec_taps, dec_bias_part)
        for late in range(2):
            if s == chunks + 1 + late:
                home = lax.dynamic_update_slice(home, arrived[late][None], (1 - ty, 0, spans[late][0], 0, 0))
        if s < chunks + 2:
            state = (sent, bufs, fronts, home, away, arrived, dec_total, grad, enc_total, dec_flat, there, lent)
            state = lax.optimization_barrier(state)
            got, bufs, fronts, home, away, arrived, dec_total, grad, enc_total, dec_flat, there, lent = state
    enc_weight_grad, dec_weight_grad, enc_bias_grad, dec_bias_grad = reduce(
        enc_taps.reshape(25, MID * FINE), enc_total, *dec_flat
    )
    enc_bias_grad, dec_bias_grad = enc_bias_grad[0, MID:], dec_bias_grad[0, :FINE]
    decoded = home.reshape(cotangent.shape)
    return (decoded, grad, enc_weight_grad, enc_bias_grad, dec_weight_grad, dec_bias_grad)


def solution(mesh):
    return jax.shard_map(
        body,
        mesh=mesh,
        in_specs=(
            P(("ga", "ty", "tx"), None, None),
            P("ga"),
            P(),
            P(),
            P(),
            P(),
            P("ga", None, "ty", "tx", None),
        ),
        out_specs=(
            P("ga", None, "ty", "tx", None),
            P(("ga", "ty", "tx"), None, None),
            P(),
            P(),
            P(),
            P(),
        ),
        check_vma=False,
    )
```
